32 devices in a mesh: groups: 2 (over y), patch: 4 (over z), zbin: 2 (over x), freq: 2 (over core).
Axes of the slice: x: 2, y: 2, z: 4, core: 2. Of those that a mesh axis runs over, the one named last changes fastest.
Arguments:
- density_maps: bfloat16 [8, 4, 1024, 1024], P(('groups', 'patch'), 'zbin', None, 'freq'), parts along dimension 0, may hold values from -6 to 6
- margin_src: int32 [8, 4], P('groups'), parts along dimension 0, may hold values from 0 to 7, as said below
- margin_row: int32 [8, 4], P('groups'), parts along dimension 0, may hold values from 0 to 992
- margin_count: int32 [8], P('groups'), parts along dimension 0, may hold values from 1 to 4
- class_id: int32 [8], P('groups'), parts along dimension 0, may hold values from 0 to 3
- coupling_bank: float32 [4, 128, 128], P('patch'), may hold values from -0.5 to 2
- band_edges: int32 [129], replicated, may hold values from 1 to 511, as said below
Outputs:
- spectra: float32 [8, 10, 128], P(('groups', 'patch'), 'zbin'), parts along dimension 0
The draws below stay inside these ranges and needn't reach their ends.
There are 2 independent parts, one for each index of `groups`. The reference program is written for one: setup_inputs(seed, part) draws one part's arguments, and reference() takes and returns one part's arrays. A program takes and returns all parts, laid end to end along the dimension named above; an argument that names none is the same for every part. Nothing has to cross between parts.
Inputs may be any that keep to these rules, and one draw needn't show every extreme that they name: `margin_src`: entry k of patch p names strip 2 q + s, side s of patch q, where q lies 1 to 1 patches away from p, counted cyclically over the 4 patches. `band_edges`: strictly increasing, the first 1 and the last half of 1024 minus 1.
All inputs are finite; a program needn't handle non-finite values.
Results may differ from the reference program's by a relative error of at most 0.0011.
Values may be sent and summed in bfloat16 or wider, within the bound.
A program may use at most 64 MiB of HBM per device.

```python
import math
import jax
import jax.numpy as jnp
import numpy as np
from jax import lax

P_SIZE = 1024
BINS = 4
NPAIR = 10
PATCH_DEV = 1
PATCHES = 4
W = 32
APOD = 64
KMAX = 4
NBAND = 128
CLASS_DEV = 1
NCLASS = 4


def draw_density_maps(key, part):
    key = jax.random.fold_in(key, 21)
    key_common, key_own, key_amp = jax.random.split(key, 3)
    log_amp = jax.random.uniform(key_amp, (1, BINS, 1, 1), jnp.float32, math.log(0.5), math.log(2.0))
    amplitude = jnp.exp(log_amp)
    common = jax.random.normal(key_common, (PATCHES, 1, P_SIZE, P_SIZE), jnp.float32)
    own = jax.random.normal(key_own, (PATCHES, BINS, P_SIZE, P_SIZE), jnp.float32)
    field = amplitude * (0.7 * common + 0.7 * own)
    return jnp.clip(field, -6.0, 6.0).astype(jnp.bfloat16)


def draw_margin_src(key, part):
    key = jax.random.fold_in(key, 11)
    key_dist, key_sign, key_side = jax.random.split(key, 3)
    distance = jax.random.randint(key_dist, (PATCHES, KMAX), 1, PATCH_DEV + 1)
    direction = 2 * jax.random.randint(key_sign, (PATCHES, KMAX), 0, 2) - 1
    strip_side = jax.random.randint(key_side, (PATCHES, KMAX), 0, 2)
    distance = distance.at[0, 0].set(PATCH_DEV)
    patch_index = jnp.arange(PATCHES, dtype=jnp.int32)[:, None]
    source = (patch_index + direction * distance) % PATCHES
    return (2 * source + strip_side).astype(jnp.int32)


def draw_margin_row(key, part):
    key = jax.random.fold_in(key, 13)
    rows = jax.random.randint(key, (PATCHES, KMAX), 0, P_SIZE - W + 1)
    rows = rows.at[0, 0].set(0)
    rows = rows.at[PATCHES - 1, 0].set(P_SIZE - W)
    return rows.astype(jnp.int32)


def draw_margin_count(key, part):
    key = jax.random.fold_in(key, 17)
    counts = jax.random.randint(key, (PATCHES,), 1, KMAX + 1)
    counts = counts.at[0].set(KMAX)
    counts = counts.at[PATCHES - 1].set(1)
    return counts.astype(jnp.int32)


def draw_class_id(key, part):
    key = jax.random.fold_in(key, 19)
    key_a, key_b, key_perm, key_pick, key_swap = jax.random.split(key, 5)
    first = jax.random.randint(key_a, (PATCHES,), 0, NCLASS)
    second = jax.random.randint(key_b, (PATCHES,), 0, NCLASS)
    ranked = jnp.minimum(first, second)
    order = jax.random.permutation(key_perm, NCLASS).astype(jnp.int32)
    chosen = jnp.sum(jnp.where(ranked[:, None] == jnp.arange(NCLASS)[None, :], order[None, :], 0), axis=1)
    owners = NCLASS // CLASS_DEV
    patch_pick = jax.random.randint(key_pick, (), 0, PATCHES)
    if PATCHES >= 8:
        device_now = patch_pick // PATCH_DEV
        before = (device_now + owners - 1) % owners * CLASS_DEV
        chosen = chosen.at[patch_pick].set(before)
        other_patch = (patch_pick + PATCHES // 2 + PATCH_DEV) % PATCHES
        other_device = other_patch // PATCH_DEV
        across = (other_device + owners // 2) % owners * CLASS_DEV
        chosen = chosen.at[other_patch].set(across)
    swapped = jax.random.randint(key_swap, (), 0, 2)
    low_value = swapped * (NCLASS - 1)
    high_value = (1 - swapped) * (NCLASS - 1)
    chosen = chosen.at[(patch_pick + 1) % PATCHES].set(low_value)
    chosen = chosen.at[(patch_pick + 2) % PATCHES].set(high_value)
    return chosen.astype(jnp.int32)


def draw_coupling_bank(key, part):
    key = jax.random.fold_in(key, 31)
    key_diag, key_off = jax.random.split(key, 2)
    diagonal = 1.0 + jax.random.uniform(key_diag, (NCLASS, NBAND), jnp.float32, 0.0, 1.0)
    spread = jax.random.normal(key_off, (NCLASS, NBAND, NBAND), jnp.float32) * (0.6 / math.sqrt(NBAND))
    spread = jnp.clip(spread, -0.5, 0.5)
    identity = (jnp.arange(NBAND)[:, None] == jnp.arange(NBAND)[None, :]).astype(jnp.float32)
    return (spread * (1.0 - identity)[None] + diagonal[:, :, None] * identity[None]).astype(jnp.float32)


def draw_band_edges(key, part):
    key = jax.random.fold_in(key, 41)
    inner = jax.random.permutation(key, P_SIZE // 2 - 3) + 2
    chosen = jnp.sort(inner[:NBAND - 1]).astype(jnp.int32)
    first_edge = jnp.array([1], dtype=jnp.int32)
    last_edge = jnp.array([P_SIZE // 2 - 1], dtype=jnp.int32)
    return jnp.concatenate([first_edge, chosen, last_edge])


def setup_inputs(seed: int = 0, part: int = 0) -> dict:
    keys = jax.random.split(jax.random.key(seed), 8)
    own_keys = jax.random.split(jax.random.fold_in(keys[7], part), 8)
    density_maps = draw_density_maps(jax.random.fold_in(jax.random.fold_in(keys[7], part), 71), part)
    margin_src = draw_margin_src(jax.random.fold_in(jax.random.fold_in(keys[7], part), 71), part)
    margin_row = draw_margin_row(jax.random.fold_in(jax.random.fold_in(keys[7], part), 71), part)
    margin_count = draw_margin_count(jax.random.fold_in(jax.random.fold_in(keys[7], part), 71), part)
    class_id = draw_class_id(jax.random.fold_in(jax.random.fold_in(keys[7], part), 71), part)
    coupling_bank = draw_coupling_bank(jax.random.fold_in(keys[7], 71), part)
    band_edges = draw_band_edges(jax.random.fold_in(keys[7], 71), part)
    return dict(density_maps=density_maps, margin_src=margin_src, margin_row=margin_row, margin_count=margin_count, class_id=class_id, coupling_bank=coupling_bank, band_edges=band_edges)


def taper_profile(length, ramp_width):
    position = jnp.arange(length, dtype=jnp.int32)
    distance = jnp.minimum(position, length - 1 - position)
    ramped = 0.5 - 0.5 * jnp.cos(math.pi * (distance.astype(jnp.float32) + 0.5) / ramp_width)
    return jnp.where(distance < ramp_width, ramped, jnp.ones_like(ramped))


def fourier_tables(frequencies, samples, length):
    phases = (frequencies[:, None] * samples[None, :]) % length
    angles = phases.astype(jnp.float32) * (2.0 * math.pi / length)
    return jnp.cos(angles).astype(jnp.bfloat16), jnp.sin(angles).astype(jnp.bfloat16)


def band_table(wave_rows, length, band_edges):
    wave_cols = jnp.arange(length, dtype=jnp.int32)
    folded = jnp.where(wave_cols < length // 2, wave_cols, wave_cols - length)
    radius_squared = (wave_rows[:, None] * wave_rows[:, None] + folded[None, :] * folded[None, :]).reshape(-1)
    edge_squared = band_edges * band_edges
    inside = (radius_squared[:, None] >= edge_squared[None, :-1]) & (radius_squared[:, None] < edge_squared[None, 1:])
    return inside.astype(jnp.float32)


def mode_counts(band_edges, length):
    halfway = length // 2
    wave_rows = jnp.arange(halfway, dtype=jnp.int32)
    wave_abs = jnp.arange(halfway + 1, dtype=jnp.int32)
    weights = jnp.where((wave_abs == 0) | (wave_abs == halfway), 1, 2).astype(jnp.int32)
    radius_squared = wave_rows[:, None] * wave_rows[:, None] + wave_abs[None, :] * wave_abs[None, :]

    def below_edge(edge_value):
        return jnp.sum(jnp.where(radius_squared < edge_value * edge_value, weights[None, :], 0).astype(jnp.int32))

    totals = lax.map(below_edge, band_edges)
    return (totals[1:] - totals[:-1]).astype(jnp.float32)


def rounded(values):
    return lax.optimization_barrier(values.astype(jnp.bfloat16)).astype(jnp.float32)


def reference(density_maps, margin_src, margin_row, margin_count, class_id, coupling_bank, band_edges):
    highest = lax.Precision.HIGHEST
    tops = density_maps[:, :, :W, :]
    bottoms = density_maps[:, :, P_SIZE - W:, :]
    strip_bank = jnp.stack([tops, bottoms], axis=1).reshape(2 * PATCHES, BINS, W, P_SIZE)
    profile = taper_profile(P_SIZE, APOD)
    pixel_index = jnp.arange(P_SIZE, dtype=jnp.int32)
    cos_rows, sin_rows = fourier_tables(jnp.arange(P_SIZE // 2, dtype=jnp.int32), pixel_index, P_SIZE)
    cos_full, sin_full = fourier_tables(pixel_index, pixel_index, P_SIZE)
    cos_rows = cos_rows.astype(jnp.float32)
    sin_rows = sin_rows.astype(jnp.float32)
    cos_full = cos_full.astype(jnp.float32)
    sin_full = sin_full.astype(jnp.float32)
    first_np, second_np = np.triu_indices(BINS)
    first_bin = jnp.asarray(first_np, dtype=jnp.int32)
    second_bin = jnp.asarray(second_np, dtype=jnp.int32)
    counts = mode_counts(band_edges, P_SIZE)
    block_rows = math.gcd(P_SIZE // 2, 16)

    def one_patch(patch_now):
        image = density_maps[patch_now].astype(jnp.float32)
        for entry_index in range(KMAX):
            strip_id = margin_src[patch_now, entry_index]
            live = (entry_index < margin_count[patch_now]).astype(jnp.float32)
            chosen = strip_bank[strip_id].astype(jnp.float32) * live
            row_at = margin_row[patch_now, entry_index].astype(jnp.int32)
            anchor = (jnp.int32(0), row_at, jnp.int32(0))
            current = lax.dynamic_slice(image, anchor, (BINS, W, P_SIZE))
            image = lax.dynamic_update_slice(image, current + chosen, anchor)
        tapered = rounded(image * profile[None, :, None] * profile[None, None, :])
        cols_real = rounded(jnp.einsum("ky,byx->bkx", cos_rows, tapered, precision=highest))
        cols_imag = rounded(-jnp.einsum("ky,byx->bkx", sin_rows, tapered, precision=highest))
        modes_real = rounded(jnp.einsum("bkx,xf->bkf", cols_real, cos_full, precision=highest)
                             + jnp.einsum("bkx,xf->bkf", cols_imag, sin_full, precision=highest))
        modes_imag = rounded(jnp.einsum("bkx,xf->bkf", cols_imag, cos_full, precision=highest)
                             - jnp.einsum("bkx,xf->bkf", cols_real, sin_full, precision=highest))

        def visit_block(running, block_index):
            offset = block_index * block_rows
            real_rows = lax.dynamic_slice_in_dim(modes_real, offset, block_rows, 1)
            imag_rows = lax.dynamic_slice_in_dim(modes_imag, offset, block_rows, 1)
            cross_terms = real_rows[first_bin] * real_rows[second_bin] + imag_rows[first_bin] * imag_rows[second_bin]
            wave_rows = offset + jnp.arange(block_rows, dtype=jnp.int32)
            indicator = band_table(wave_rows, P_SIZE, band_edges)
            summed = jnp.dot(cross_terms.reshape(NPAIR, block_rows * P_SIZE), indicator, precision=highest)
            return running + summed, None

        initial = jnp.zeros((NPAIR, NBAND), jnp.float32)
        totals, unused = lax.scan(visit_block, initial, jnp.arange((P_SIZE // 2) // block_rows, dtype=jnp.int32))
        pseudo = totals / (counts * float(P_SIZE * P_SIZE))[None, :]
        matrix = coupling_bank[class_id[patch_now]]
        return jnp.dot(pseudo, matrix.T, precision=highest)

    return lax.map(one_patch, jnp.arange(PATCHES, dtype=jnp.int32))
```

```python
import math

import jax
import jax.numpy as jnp
import ml_dtypes
import numpy as np
from jax import lax
from jax.experimental import pallas as pl
from jax.experimental.pallas import tpu as pltpu
from jax.sharding import PartitionSpec as P

W = 32
APOD = 64
LANES = 128
VMEM = pl.BlockSpec(memory_space=pltpu.VMEM)
PARAMS = dict(vmem_limit_bytes=48 * 1024 * 1024)


def taper_profile(length, ramp_width):
    position = np.arange(length)
    distance = np.minimum(position, length - 1 - position)
    ramped = 0.5 - 0.5 * np.cos(math.pi * (distance + 0.5) / ramp_width)
    return np.where(distance < ramp_width, ramped, 1.0).astype(np.float32)


def fourier_tables(length):
    half = length // 2
    phases = np.arange(half)[:, None] * np.arange(length)[None, :] % length
    angles = phases * (2.0 * math.pi / length)
    return (
        np.cos(angles).astype(np.float32).astype(ml_dtypes.bfloat16),
        np.sin(angles).astype(np.float32).astype(ml_dtypes.bfloat16),
    )


def edge_reach(edge_squared, wave_rows):
    room = edge_squared - wave_rows * wave_rows
    reach = jnp.sqrt(jnp.maximum(room, 0).astype(jnp.float32)).astype(jnp.int32) - 1
    for _ in range(3):
        reach = reach + (reach * reach < room).astype(jnp.int32)
    return jnp.where(room > 0, reach, 0)


def first_kernel(maps_ref, strips_ref, pick_ref, row_taper_ref, col_taper_ref, table_ref, out_ref, tapered):
    bins, length, columns = maps_ref.shape
    block = 256

    @pl.when(pl.program_id(0) == 0)
    def _():
        for b in range(bins):
            for r in range(0, length, block):
                rows = pl.ds(r, block)
                image = maps_ref[b, rows, :].astype(jnp.float32) + jnp.dot(
                    pick_ref[rows, :], strips_ref[b], preferred_element_type=jnp.float32
                )
                tapered[b, rows, :] = (image * row_taper_ref[rows, :] * col_taper_ref[...]).astype(jnp.bfloat16)

    for b in range(bins):
        out_ref[0, 0, b] = jnp.dot(table_ref[...], tapered[b], preferred_element_type=jnp.float32).astype(jnp.bfloat16)


def second_kernel(cols_ref, cos_ref, sin_ref, out_ref):
    sources, _, _, _, columns = cols_ref.shape

    def product(part, table_ref):
        total = None
        for s in range(sources):
            term = jnp.dot(
                cols_ref[s, part, 0],
                table_ref[pl.ds(s * columns, columns), :],
                preferred_element_type=jnp.float32,
            )
            total = term if total is None else total + term
        return total

    real_cos, imag_sin = product(0, cos_ref), product(1, sin_ref)
    out_ref[0, 0, 0] = (real_cos + imag_sin).astype(jnp.bfloat16)
    out_ref[0, 0, 1] = (real_cos - imag_sin).astype(jnp.bfloat16)
    imag_cos, real_sin = product(1, cos_ref), product(0, sin_ref)
    out_ref[0, 0, 2] = (imag_cos - real_sin).astype(jnp.bfloat16)
    out_ref[0, 0, 3] = (imag_cos + real_sin).astype(jnp.bfloat16)


def band_kernel(pairs, modes_ref, row_ref, edges_ref, low_ref, prefix_ref, out_ref):
    _, local, _, rows, half = modes_ref.shape
    wave_rows = row_ref[0, 0] + lax.broadcasted_iota(jnp.int32, (rows, LANES), 0)
    lane = lax.broadcasted_iota(jnp.int32, (rows, LANES), 1)
    edges = edges_ref[...]
    reach = edge_reach(edges * edges, wave_rows)
    low = low_ref[0, 0]
    weight = jnp.where(lane == 0, 0.5, 1.0)
    prefix = prefix_ref[...]
    out_ref[...] = jnp.zeros_like(out_ref)
    for b in range(half // LANES):
        columns = pl.ds(b * LANES, LANES)
        index = jnp.clip(reach - b * LANES, 1, LANES) - 1
        inside = reach > b * LANES
        wave_cols = lane + b * LANES
        scale = (wave_rows * wave_rows + wave_cols * wave_cols >= low * low).astype(jnp.float32)
        if b == 0:
            scale = scale * weight
        for n, (i, j) in enumerate(pairs):
            cross = None
            for c in range(4):
                term = modes_ref[i // local, i % local, c, :, columns].astype(jnp.float32) * modes_ref[
                    j // local, j % local, c, :, columns
                ].astype(jnp.float32)
                cross = term if cross is None else cross + term
            cross = cross * scale
            upper = cross.astype(jnp.bfloat16)
            lower = (cross - upper.astype(jnp.float32)).astype(jnp.bfloat16)
            sums = jnp.dot(
                jnp.concatenate([upper, lower], axis=1), prefix, preferred_element_type=jnp.float32
            )
            taken = jnp.where(inside, jnp.take_along_axis(sums, index, axis=1), 0.0)
            out_ref[pl.ds(n, 1), :] += jnp.sum(taken, axis=0, keepdims=True)


def per_device(density_maps, margin_src, margin_row, margin_count, class_id, coupling_bank, band_edges):
    _, bins_local, length, columns = density_maps.shape
    half = length // 2
    freq_count = lax.axis_size("freq")
    zbin_count = lax.axis_size("zbin")
    patch_count = lax.axis_size("patch")
    bins_total = bins_local * zbin_count
    me = lax.axis_index("patch")
    rows_freq = half // freq_count
    rows_zbin = rows_freq // zbin_count

    maps = density_maps[0]
    strips = jnp.concatenate([maps[:, :W, :], maps[:, length - W :, :]], axis=1)
    from_left = lax.ppermute(strips, "patch", [(i, (i + 1) % patch_count) for i in range(patch_count)])
    from_right = lax.ppermute(strips, "patch", [((i + 1) % patch_count, i) for i in range(patch_count)])
    nearby = jnp.concatenate([from_left, from_right], axis=1)

    source = margin_src[me]
    side = jnp.where(source // 2 == (me + patch_count - 1) % patch_count, 0, 1)
    slot = (side * 2 + source % 2) * W
    live = jnp.arange(source.shape[0]) < margin_count[me]
    pixel = jnp.arange(length, dtype=jnp.int32)[:, None, None]
    place = jnp.arange(4 * W, dtype=jnp.int32)[None, :, None]
    strip_row = place - slot[None, None, :]
    hit = (strip_row >= 0) & (strip_row < W) & (pixel == margin_row[me][None, None, :] + strip_row) & live[None, None, :]
    pick = jnp.sum(hit.astype(jnp.float32), axis=2).astype(jnp.bfloat16)

    profile = taper_profile(length, APOD)
    col_taper = lax.dynamic_slice_in_dim(jnp.asarray(profile), lax.axis_index("freq") * columns, columns, 0)
    cos_np, sin_np = fourier_tables(length)
    minus_sin = (-sin_np.astype(np.float32)).astype(ml_dtypes.bfloat16)
    table = jnp.asarray(np.concatenate([cos_np, minus_sin], axis=0))
    cols = pl.pallas_call(
        first_kernel,
        grid=(2 * freq_count,),
        out_shape=jax.ShapeDtypeStruct((freq_count, 2, bins_local, rows_freq, columns), jnp.bfloat16),
        in_specs=[VMEM] * 5 + [pl.BlockSpec((rows_freq, length), lambda i: (i, 0))],
        out_specs=pl.BlockSpec(
            (1, 1, bins_local, rows_freq, columns), lambda i: (i % freq_count, i // freq_count, 0, 0, 0)
        ),
        scratch_shapes=[pltpu.VMEM((bins_local, length, columns), jnp.bfloat16)],
        compiler_params=pltpu.CompilerParams(**PARAMS),
        name="first_transform",
    )(maps, nearby, pick, jnp.asarray(profile)[:, None], col_taper[None, :], table)

    cols = lax.all_to_all(cols, "freq", split_axis=0, concat_axis=0, tiled=True)

    modes = pl.pallas_call(
        second_kernel,
        grid=(zbin_count, bins_local),
        out_shape=jax.ShapeDtypeStruct((zbin_count, bins_local, 4, rows_zbin, half), jnp.bfloat16),
        in_specs=[
            pl.BlockSpec((freq_count, 2, 1, rows_zbin, columns), lambda z, b: (0, 0, b, z, 0)),
            VMEM,
            VMEM,
        ],
        out_specs=pl.BlockSpec((1, 1, 4, rows_zbin, half), lambda z, b: (z, b, 0, 0, 0)),
        compiler_params=pltpu.CompilerParams(**PARAMS),
        name="second_transform",
    )(cols, jnp.asarray(np.ascontiguousarray(cos_np.T)), jnp.asarray(np.ascontiguousarray(sin_np.T)))

    modes = lax.all_to_all(modes, "zbin", split_axis=0, concat_axis=0, tiled=True)

    first_np, second_np = np.triu_indices(bins_total)
    pairs = [(int(i), int(j)) for i, j in zip(first_np, second_np)]
    row_start = lax.axis_index("freq") * rows_freq + lax.axis_index("zbin") * rows_zbin
    ones = np.triu(np.ones((LANES, LANES)))
    prefix = jnp.asarray(np.concatenate([ones, ones], axis=0).astype(ml_dtypes.bfloat16))
    smem = pl.BlockSpec(memory_space=pltpu.SMEM)
    discs = pl.pallas_call(
        lambda *refs: band_kernel(pairs, *refs),
        out_shape=jax.ShapeDtypeStruct((len(pairs), LANES), jnp.float32),
        in_specs=[VMEM, smem, VMEM, smem, VMEM],
        out_specs=VMEM,
        compiler_params=pltpu.CompilerParams(**PARAMS),
        name="band_sums",
    )(modes, row_start.reshape(1, 1), band_edges[None, 1:], band_edges[:1].reshape(1, 1), prefix)

    share = lax.psum_scatter(discs, "zbin", scatter_dimension=0, tiled=True)
    share = lax.psum(share, "freq")
    totals = share - jnp.pad(share, ((0, 0), (1, 0)))[:, :-1]

    reach = edge_reach(
        (band_edges * band_edges)[None, :], jnp.arange(half, dtype=jnp.int32)[:, None]
    )
    below = jnp.sum(jnp.maximum(2 * reach - 1, 0), axis=0)
    counts = (below[1:] - below[:-1]).astype(jnp.float32)
    pseudo = totals / (counts * float(length * length))[None, :]
    bank = lax.all_gather(coupling_bank, "patch", axis=0, tiled=True)
    matrix = lax.dynamic_index_in_dim(bank, class_id[me], 0, keepdims=False)
    return jnp.einsum("qb,ab->qa", pseudo, matrix, precision=lax.Precision.HIGHEST)[None]


def solution(mesh):
    in_specs = (
        P(("groups", "patch"), "zbin", None, "freq"),
        P("groups", None),
        P("groups", None),
        P("groups"),
        P("groups"),
        P("patch", None, None),
        P(),
    )
    out_specs = P(("groups", "patch"), "zbin", None)
    return jax.shard_map(
        per_device, mesh=mesh, in_specs=in_specs, out_specs=out_specs, check_vma=False
    )
```

```python
import math

import jax
import jax.numpy as jnp
import ml_dtypes
import numpy as np
from jax import lax
from jax.experimental import pallas as pl
from jax.experimental.pallas import tpu as pltpu
from jax.sharding import PartitionSpec as P

W = 32
APOD = 64
LANES = 128
MESH = pl.DeviceIdType.MESH


def taper_profile(length, ramp_width):
    position = np.arange(length)
    distance = np.minimum(position, length - 1 - position)
    ramped = 0.5 - 0.5 * np.cos(math.pi * (distance + 0.5) / ramp_width)
    return np.where(distance < ramp_width, ramped, 1.0).astype(np.float32)


def fourier_tables(length):
    half = length // 2
    phases = np.arange(half)[:, None] * np.arange(length)[None, :] % length
    angles = phases * (2.0 * math.pi / length)
    return (
        np.cos(angles).astype(np.float32).astype(ml_dtypes.bfloat16),
        np.sin(angles).astype(np.float32).astype(ml_dtypes.bfloat16),
    )


def edge_reach(edges, wave_rows):
    room = edges * edges - wave_rows * wave_rows
    reach = jnp.sqrt(jnp.maximum(room, 0).astype(jnp.float32)).astype(jnp.int32) - 1
    for _ in range(3):
        reach = reach + (reach * reach < room).astype(jnp.int32)
    return jnp.where(room > 0, reach, 0)


def kernel(
    sizes,
    src_ref, row_ref, count_ref, class_ref, edges_ref, ramp_ref, col_taper_ref, prefix_ref,
    maps_hbm, bank_hbm, table_hbm, turn_hbm,
    out_ref,
    maps, table, turn, strips, bank, tapered,
    cols_send, cols_own, cols_recv, modes_send, modes, discs, shares,
    load_sem, strip_send, strip_recv, bank_send, bank_recv, cols_ssem, cols_rsem,
    modes_ssem, modes_rsem, share_ssem, share_rsem,
):
    patches, zbins, freqs = sizes
    bins, length, columns = maps.shape
    half = length // 2
    rows_freq = half // freqs
    rows = rows_freq // zbins
    bins_total = bins * zbins
    pair_total = bins_total * (bins_total + 1) // 2
    pair_share = pair_total // zbins
    me = lax.axis_index("patch")
    z = lax.axis_index("zbin")
    f = lax.axis_index("freq")
    other = 1 - f
    right, left = lax.rem(me + 1, patches), lax.rem(me + patches - 1, patches)

    loads = [
        pltpu.make_async_copy(maps_hbm.at[0], maps, load_sem.at[0]),
        pltpu.make_async_copy(table_hbm, table, load_sem.at[1]),
        pltpu.make_async_copy(turn_hbm, turn, load_sem.at[2]),
        pltpu.make_async_copy(bank_hbm, bank.at[0], load_sem.at[3]),
    ]
    for load in loads:
        load.start()

    group = [(dz, df) for dz in range(zbins) for df in range(freqs) if (dz, df) != (0, 0)]
    barrier = pltpu.get_barrier_semaphore()
    for k in range(1, patches):
        pl.semaphore_signal(barrier, inc=1, device_id={"patch": lax.rem(me + k, patches)}, device_id_type=MESH)
    for dz, df in group:
        pl.semaphore_signal(
            barrier,
            inc=1,
            device_id={"zbin": lax.rem(z + dz, zbins), "freq": lax.rem(f + df, freqs)},
            device_id_type=MESH,
        )
    pl.semaphore_wait(barrier, patches - 1 + len(group))

    strip_copies = []
    for side, target in ((0, right), (1, left)):
        for s, at in ((0, 0), (1, length - W)):
            slot = side * 2 + s
            copy = pltpu.make_async_remote_copy(
                src_ref=maps_hbm.at[0, :, pl.ds(at, W), :],
                dst_ref=strips.at[:, slot],
                send_sem=strip_send.at[slot],
                recv_sem=strip_recv.at[slot],
                device_id={"patch": target},
                device_id_type=MESH,
            )
            copy.start()
            strip_copies.append(copy)

    discs[...] = jnp.zeros_like(discs)
    entries = []
    for k in range(src_ref.shape[1]):
        source = src_ref[me, k]
        side = jnp.where(lax.shift_right_logical(source, 1) == left, 0, 1)
        slot = (side * 2 + (source & 1)) * W
        live = k < count_ref[me]
        entries.append((jnp.where(live, slot, -length), row_ref[me, k]))
    place = lax.broadcasted_iota(jnp.int32, (1, 4 * W), 1)
    marks = []
    for slot, row in entries:
        at = place - slot
        marks.append(jnp.where((at >= 0) & (at < W), at + row, -1))

    loads[0].wait()
    for copy in strip_copies:
        copy.wait_recv()

    bank_copies = []
    for k in range(1, patches):
        copy = pltpu.make_async_remote_copy(
            src_ref=bank_hbm,
            dst_ref=bank.at[k],
            send_sem=bank_send.at[k],
            recv_sem=bank_recv.at[k],
            device_id={"patch": lax.rem(me + k, patches)},
            device_id_type=MESH,
        )
        copy.start()
        bank_copies.append(copy)

    col_taper = col_taper_ref[:, pl.ds(pl.multiple_of(f * columns, columns), columns)]
    bounds = [0, APOD] + list(range(4 * APOD, length - APOD, 4 * APOD)) + [length - APOD, length]
    for start, stop in zip(bounds[:-1], bounds[1:]):
        pixel = start + lax.broadcasted_iota(jnp.int32, (stop - start, 1), 0)
        pick = None
        for mark in marks:
            hit = (pixel == mark).astype(jnp.float32)
            pick = hit if pick is None else pick + hit
        pick = pick.astype(jnp.bfloat16)
        for b in range(bins):
            image = maps[b, pl.ds(start, stop - start), :].astype(jnp.float32) + jnp.dot(
                pick, strips[b].reshape(4 * W, columns), preferred_element_type=jnp.float32
            )
            if start == 0:
                image = image * ramp_ref[pl.ds(0, APOD), :]
            if stop == length:
                image = image * ramp_ref[pl.ds(APOD, APOD), :]
            tapered[b, pl.ds(start, stop - start), :] = (image * col_taper).astype(jnp.bfloat16)

    order = list(range(1, zbins)) + [0]
    loads[1].wait()

    def first_transform(half_index, d, target):
        base = half_index * rows_freq + lax.rem(z + d, zbins) * rows
        lhs = jnp.concatenate(
            [
                table[pl.ds(pl.multiple_of(base, rows), rows), :],
                table[pl.ds(pl.multiple_of(half + base, rows), rows), :],
            ],
            axis=0,
        )
        for b in range(bins):
            target[d, b] = jnp.dot(lhs, tapered[b], preferred_element_type=jnp.float32).astype(jnp.bfloat16)

    cols_copies = {}
    for d in order:
        first_transform(other, d, cols_send)
        copy = pltpu.make_async_remote_copy(
            src_ref=cols_send.at[d],
            dst_ref=cols_recv.at[d],
            send_sem=cols_ssem.at[d],
            recv_sem=cols_rsem.at[d],
            device_id={"freq": other},
            device_id_type=MESH,
        )
        copy.start()
        cols_copies[d] = copy

    def second_transform(d, b, store):
        own = pl.ds(pl.multiple_of(f * columns, columns), columns)
        far = pl.ds(pl.multiple_of(other * columns, columns), columns)
        both = [
            jnp.dot(cols_own[d, b], turn[t, own, :], preferred_element_type=jnp.float32)
            + jnp.dot(cols_recv[d, b], turn[t, far, :], preferred_element_type=jnp.float32)
            for t in range(2)
        ]
        real_cos, imag_cos = both[0][:rows], both[0][rows:]
        real_sin, imag_sin = both[1][:rows], both[1][rows:]
        store(0, (real_cos + imag_sin).astype(jnp.bfloat16))
        store(1, (real_cos - imag_sin).astype(jnp.bfloat16))
        store(2, (imag_cos - real_sin).astype(jnp.bfloat16))
        store(3, (imag_cos + real_sin).astype(jnp.bfloat16))

    modes_copies = {}
    for d in order:
        first_transform(f, d, cols_own)
        if d == order[0]:
            loads[2].wait()
        cols_copies[d].wait_recv()
        for b in range(bins):
            buffer = modes_send if d else modes

            def store(part, value, buffer=buffer, d=d, b=b):
                buffer[d, b, part] = value

            second_transform(d, b, store)
            if d:
                copy = pltpu.make_async_remote_copy(
                    src_ref=modes_send.at[d, b],
                    dst_ref=modes.at[d, b],
                    send_sem=modes_ssem.at[d, b],
                    recv_sem=modes_rsem.at[d, b],
                    device_id={"zbin": lax.rem(z + d, zbins)},
                    device_id_type=MESH,
                )
                copy.start()
                modes_copies[d, b] = copy

    wave_rows = f * rows_freq + z * rows + lax.broadcasted_iota(jnp.int32, (rows, LANES), 0)
    lane = lax.broadcasted_iota(jnp.int32, (rows, LANES), 1)
    lower_edges = edges_ref[pl.ds(0, 1), :]
    upper_edges = edges_ref[pl.ds(1, 1), :]
    low = lower_edges[:, :1]
    reach = edge_reach(upper_edges, wave_rows)

    def band_sums(pairs):
        for block in range(half // LANES):
            lanes = pl.ds(block * LANES, LANES)
            index = jnp.clip(reach - block * LANES, 1, LANES) - 1
            inside = reach > block * LANES
            wave_cols = lane + block * LANES
            scale = (wave_rows * wave_rows + wave_cols * wave_cols >= low * low).astype(jnp.float32)
            if block == 0:
                scale = scale * jnp.where(lane == 0, 0.5, 1.0)
            for (d1, b1), (d2, b2) in pairs:
                cross = None
                for c in range(4):
                    term = modes[d1, b1, c, :, lanes].astype(jnp.float32) * modes[
                        d2, b2, c, :, lanes
                    ].astype(jnp.float32)
                    cross = term if cross is None else cross + term
                cross = cross * scale
                upper = cross.astype(jnp.bfloat16)
                lower = (cross - upper.astype(jnp.float32)).astype(jnp.bfloat16)
                sums = jnp.dot(
                    jnp.concatenate([upper, lower], axis=1), prefix_ref[...], preferred_element_type=jnp.float32
                )
                taken = jnp.where(inside, jnp.take_along_axis(sums, index, axis=1), 0.0)
                g1 = lax.rem(z + zbins - d1, zbins) * bins + b1
                g2 = lax.rem(z + zbins - d2, zbins) * bins + b2
                first, second = jnp.minimum(g1, g2), jnp.maximum(g1, g2)
                number = first * bins_total - first * (first - 1) // 2 + second - first
                spot = number // pair_share
                line = pl.ds(number - spot * pair_share, 1)
                discs[spot, line, :] += jnp.sum(taken, axis=0, keepdims=True)

    bins_of = {d: [(d, b) for b in range(bins)] for d in range(zbins)}
    own = bins_of[0]
    band_sums([(own[i], own[j]) for i in range(bins) for j in range(i, bins)])

    counts = jnp.zeros((1, LANES), jnp.int32)
    for start in range(0, half, LANES):
        every = start + lax.broadcasted_iota(jnp.int32, (LANES, LANES), 0)
        inner = jnp.maximum(2 * edge_reach(lower_edges, every) - 1, 0)
        outer = jnp.maximum(2 * edge_reach(upper_edges, every) - 1, 0)
        counts = counts + jnp.sum(outer - inner, axis=0, keepdims=True)

    done = list(own)
    for d in range(1, zbins):
        for b in range(bins):
            modes_copies[d, b].wait_recv()
            done.append((d, b))
            band_sums([(old, (d, b)) for old in done])
    loads[3].wait()

    copies = []
    for n, (dz, df) in enumerate(group):
        target = lax.rem(z + dz, zbins)
        copy = pltpu.make_async_remote_copy(
            src_ref=discs.at[target],
            dst_ref=shares.at[n],
            send_sem=share_ssem.at[n],
            recv_sem=share_rsem.at[n],
            device_id={"zbin": target, "freq": lax.rem(f + df, freqs)},
            device_id_type=MESH,
        )
        copy.start()
        copies.append(copy)
    total = discs[z]
    for n, copy in enumerate(copies):
        copy.wait_recv()
        total = total + shares[n]
    for copy in bank_copies:
        copy.wait_recv()

    shifted = pltpu.roll(total, 1, 1)
    shifted = jnp.where(lax.broadcasted_iota(jnp.int32, total.shape, 1) == 0, 0.0, shifted)
    pseudo = (total - shifted) / (counts.astype(jnp.float32) * float(length * length))
    kind = class_ref[me]
    holder = kind // bank.shape[1]
    matrix = bank[lax.rem(me - holder + patches, patches), kind - holder * bank.shape[1]]
    result = lax.dot_general(
        pseudo,
        matrix,
        (((1,), (1,)), ((), ())),
        precision=lax.Precision.HIGHEST,
        preferred_element_type=jnp.float32,
    )
    out_ref[0] = result[:pair_share]

    for copy in strip_copies + bank_copies + list(cols_copies.values()) + list(modes_copies.values()) + copies:
        copy.wait_send()


def per_device(density_maps, margin_src, margin_row, margin_count, class_id, coupling_bank, band_edges):
    _, bins, length, columns = density_maps.shape
    half = length // 2
    freqs = lax.axis_size("freq")
    zbins = lax.axis_size("zbin")
    patches = lax.axis_size("patch")
    rows = half // freqs // zbins
    bins_total = bins * zbins
    pair_share = bins_total * (bins_total + 1) // 2 // zbins
    padded = -(-pair_share // 8) * 8
    group = zbins * freqs - 1

    profile = taper_profile(length, APOD)
    ramp = np.concatenate([profile[:APOD], profile[length - APOD :]])[:, None]
    cos_np, sin_np = fourier_tables(length)
    minus_sin = (-sin_np.astype(np.float32)).astype(ml_dtypes.bfloat16)
    table = np.concatenate([cos_np, minus_sin], axis=0)
    turn = np.stack([np.ascontiguousarray(cos_np.T), np.ascontiguousarray(sin_np.T)])
    ones = np.triu(np.ones((LANES, LANES)))
    prefix = np.concatenate([ones, ones], axis=0).astype(ml_dtypes.bfloat16)
    edges = jnp.stack([band_edges[:-1], band_edges[1:]])

    smem = pl.BlockSpec(memory_space=pltpu.SMEM)
    vmem = pl.BlockSpec(memory_space=pltpu.VMEM)
    anywhere = pl.BlockSpec(memory_space=pl.ANY)
    dma = pltpu.SemaphoreType.DMA
    bf16, f32 = jnp.bfloat16, jnp.float32
    sizes = (patches, zbins, freqs)
    return pl.pallas_call(
        lambda *refs: kernel(sizes, *refs),
        out_shape=jax.ShapeDtypeStruct((1, pair_share, LANES), f32),
        in_specs=[smem] * 4 + [vmem] * 4 + [anywhere] * 4,
        out_specs=vmem,
        scratch_shapes=[
            pltpu.VMEM((bins, length, columns), bf16),
            pltpu.VMEM((length, length), bf16),
            pltpu.VMEM((2, length, half), bf16),
            pltpu.VMEM((bins, 4, W, columns), bf16),
            pltpu.VMEM((patches,) + coupling_bank.shape, f32),
            pltpu.VMEM((bins, length, columns), bf16),
            pltpu.VMEM((zbins, bins, 2 * rows, columns), bf16),
            pltpu.VMEM((zbins, bins, 2 * rows, columns), bf16),
            pltpu.VMEM((zbins, bins, 2 * rows, columns), bf16),
            pltpu.VMEM((zbins, bins, 4, rows, half), bf16),
            pltpu.VMEM((zbins, bins, 4, rows, half), bf16),
            pltpu.VMEM((zbins, padded, LANES), f32),
            pltpu.VMEM((group, padded, LANES), f32),
            dma((4,)), dma((4,)), dma((4,)), dma((patches,)), dma((patches,)), dma((zbins,)), dma((zbins,)),
            dma((zbins, bins)), dma((zbins, bins)), dma((group,)), dma((group,)),
        ],
        compiler_params=pltpu.CompilerParams(
            collective_id=0, has_side_effects=True, vmem_limit_bytes=56 * 1024 * 1024
        ),
        name="spectra",
    )(
        margin_src, margin_row, margin_count, class_id, edges, jnp.asarray(ramp),
        jnp.asarray(profile)[None, :], jnp.asarray(prefix),
        density_maps, coupling_bank, jnp.asarray(table), jnp.asarray(turn),
    )


def solution(mesh):
    in_specs = (
        P(("groups", "patch"), "zbin", None, "freq"),
        P("groups", None),
        P("groups", None),
        P("groups"),
        P("groups"),
        P("patch", None, None),
        P(),
    )
    out_specs = P(("groups", "patch"), "zbin", None)
    return jax.shard_map(
        per_device, mesh=mesh, in_specs=in_specs, out_specs=out_specs, check_vma=False
    )
```

```python
import math

import jax
import jax.numpy as jnp
import ml_dtypes
import numpy as np
from jax import lax
from jax.experimental import pallas as pl
from jax.experimental.pallas import tpu as pltpu
from jax.sharding import PartitionSpec as P

W = 32
BLOCK = 16
APOD = 64
LANES = 128
MESH = pl.DeviceIdType.MESH


def taper_profile(length, ramp_width):
    position = np.arange(length)
    distance = np.minimum(position, length - 1 - position)
    ramped = 0.5 - 0.5 * np.cos(math.pi * (distance + 0.5) / ramp_width)
    return np.where(distance < ramp_width, ramped, 1.0).astype(np.float32)


def fourier_tables(length):
    half = length // 2
    phases = np.arange(half)[:, None] * np.arange(length)[None, :] % length
    angles = phases * (2.0 * math.pi / length)
    return (
        np.cos(angles).astype(np.float32).astype(ml_dtypes.bfloat16),
        np.sin(angles).astype(np.float32).astype(ml_dtypes.bfloat16),
    )


def edge_reach(edges, wave_rows):
    room = edges * edges - wave_rows * wave_rows
    reach = jnp.sqrt(jnp.maximum(room, 0).astype(jnp.float32)).astype(jnp.int32) - 1
    for _ in range(3):
        reach = reach + (reach * reach < room).astype(jnp.int32)
    return jnp.where(room > 0, reach, 0)


def kernel(
    sizes,
    src_ref, row_ref, count_ref, class_ref, edges_ref, ramp_ref, col_taper_ref, prefix_ref,
    maps_hbm, bank_hbm, table_hbm, turn_hbm,
    out_ref,
    maps, table, turn, strips, bank, tapered,
    cols_send, cols_own, cols_recv, modes_send, modes, discs, shares,
    load_sem, strip_send, strip_recv, bank_send, bank_recv, cols_ssem, cols_rsem,
    modes_ssem, modes_rsem, share_ssem, share_rsem,
):
    patches, zbins, freqs = sizes
    bins, length, columns = maps.shape
    half = length // 2
    rows_freq = half // freqs
    rows = rows_freq // zbins
    bins_total = bins * zbins
    pair_total = bins_total * (bins_total + 1) // 2
    pair_share = pair_total // zbins
    me = lax.axis_index("patch")
    z = lax.axis_index("zbin")
    f = lax.axis_index("freq")
    other = 1 - f
    right, left = lax.rem(me + 1, patches), lax.rem(me + patches - 1, patches)

    loads = [
        pltpu.make_async_copy(maps_hbm.at[0], maps, load_sem.at[0]),
        pltpu.make_async_copy(table_hbm, table, load_sem.at[1]),
        pltpu.make_async_copy(turn_hbm, turn, load_sem.at[2]),
        pltpu.make_async_copy(bank_hbm, bank.at[0], load_sem.at[3]),
    ]
    for load in loads:
        load.start()

    group = [(dz, df) for dz in range(zbins) for df in range(freqs) if (dz, df) != (0, 0)]
    barrier = pltpu.get_barrier_semaphore()
    for k in range(1, patches):
        pl.semaphore_signal(barrier, inc=1, device_id={"patch": lax.rem(me + k, patches)}, device_id_type=MESH)
    for dz, df in group:
        pl.semaphore_signal(
            barrier,
            inc=1,
            device_id={"zbin": lax.rem(z + dz, zbins), "freq": lax.rem(f + df, freqs)},
            device_id_type=MESH,
        )
    pl.semaphore_wait(barrier, patches - 1 + len(group))

    strip_copies = []
    for side, target in ((0, right), (1, left)):
        for s, at in ((0, 0), (1, length - W)):
            slot = side * 2 + s
            copy = pltpu.make_async_remote_copy(
                src_ref=maps_hbm.at[0, :, pl.ds(at, W), :],
                dst_ref=strips.at[:, slot],
                send_sem=strip_send.at[slot],
                recv_sem=strip_recv.at[slot],
                device_id={"patch": target},
                device_id_type=MESH,
            )
            copy.start()
            strip_copies.append(copy)

    discs[...] = jnp.zeros_like(discs)
    entries = []
    for k in range(src_ref.shape[1]):
        source = src_ref[me, k]
        side = jnp.where(lax.shift_right_logical(source, 1) == left, 0, 1)
        slot = (side * 2 + (source & 1)) * W
        live = k < count_ref[me]
        entries.append((jnp.where(live, slot, -length), row_ref[me, k]))
    place = lax.broadcasted_iota(jnp.int32, (1, 4 * W), 1)
    marks = []
    for slot, row in entries:
        at = place - slot
        marks.append(jnp.where((at >= 0) & (at < W), at + row, -1))

    loads[0].wait()
    for copy in strip_copies:
        copy.wait_recv()

    col_taper = col_taper_ref[:, pl.ds(pl.multiple_of(f * columns, columns), columns)]
    bounds = [0, APOD] + list(range(4 * APOD, length - APOD, 4 * APOD)) + [length - APOD, length]
    for start, stop in zip(bounds[:-1], bounds[1:]):
        pixel = start + lax.broadcasted_iota(jnp.int32, (stop - start, 1), 0)
        pick = None
        for mark in marks:
            hit = (pixel == mark).astype(jnp.float32)
            pick = hit if pick is None else pick + hit
        pick = pick.astype(jnp.bfloat16)
        for b in range(bins):
            image = maps[b, pl.ds(start, stop - start), :].astype(jnp.float32) + jnp.dot(
                pick, strips[b].reshape(4 * W, columns), preferred_element_type=jnp.float32
            )
            if start == 0:
                image = image * ramp_ref[pl.ds(0, APOD), :]
            if stop == length:
                image = image * ramp_ref[pl.ds(APOD, APOD), :]
            tapered[b, pl.ds(start, stop - start), :] = (image * col_taper).astype(jnp.bfloat16)

    order = list(range(1, zbins)) + [0]
    blocks = half // LANES
    spread = freqs * zbins * BLOCK
    heights = [
        BLOCK * sum((at * LANES) ** 2 + (t * spread) ** 2 < (half - 1) ** 2 for t in range(rows // BLOCK))
        for at in range(blocks)
    ]
    loads[1].wait()

    def first_transform(half_index, d, target):
        base = half_index * rows_freq + lax.rem(z + d, zbins) * rows
        lhs = jnp.concatenate(
            [
                table[pl.ds(pl.multiple_of(base, rows), rows), :],
                table[pl.ds(pl.multiple_of(half + base, rows), rows), :],
            ],
            axis=0,
        )
        for b in range(bins):
            target[d, pl.ds(b * 2 * rows, 2 * rows), :] = jnp.dot(
                lhs, tapered[b], preferred_element_type=jnp.float32
            ).astype(jnp.bfloat16)

    def second_transform(d, at, target):
        own = pl.ds(pl.multiple_of(f * columns, columns), columns)
        far = pl.ds(pl.multiple_of(other * columns, columns), columns)
        both = jnp.dot(cols_own[d], turn[at, own, :], preferred_element_type=jnp.float32) + jnp.dot(
            cols_recv[d], turn[at, far, :], preferred_element_type=jnp.float32
        )
        for b in range(bins):
            real = both[b * 2 * rows : (2 * b + 1) * rows]
            imag = both[(2 * b + 1) * rows : (2 * b + 2) * rows]
            real_cos, real_sin = real[:, :LANES], real[:, LANES:]
            imag_cos, imag_sin = imag[:, :LANES], imag[:, LANES:]
            target[d, at, b, 0] = (real_cos + imag_sin).astype(jnp.bfloat16)
            target[d, at, b, 1] = (real_cos - imag_sin).astype(jnp.bfloat16)
            target[d, at, b, 2] = (imag_cos - real_sin).astype(jnp.bfloat16)
            target[d, at, b, 3] = (imag_cos + real_sin).astype(jnp.bfloat16)

    cols_copies, modes_copies = {}, {}
    for d in order:
        first_transform(other, d, cols_send)
        copy = pltpu.make_async_remote_copy(
            src_ref=cols_send.at[d],
            dst_ref=cols_recv.at[d],
            send_sem=cols_ssem.at[d],
            recv_sem=cols_rsem.at[d],
            device_id={"freq": other},
            device_id_type=MESH,
        )
        copy.start()
        cols_copies[d] = copy
        first_transform(f, d, cols_own)
        if d == order[0]:
            loads[2].wait()
        copy.wait_recv()
        for at in range(blocks):
            second_transform(d, at, modes_send if d else modes)
            if d:
                part = pl.ds(0, heights[at])
                copy = pltpu.make_async_remote_copy(
                    src_ref=modes_send.at[d, at, :, :, part, :],
                    dst_ref=modes.at[d, at, :, :, part, :],
                    send_sem=modes_ssem.at[d, at],
                    recv_sem=modes_rsem.at[d, at],
                    device_id={"zbin": lax.rem(z + d, zbins)},
                    device_id_type=MESH,
                )
                copy.start()
                modes_copies[d, at] = copy

    bank_copies = []
    for k in range(1, patches):
        copy = pltpu.make_async_remote_copy(
            src_ref=bank_hbm,
            dst_ref=bank.at[k],
            send_sem=bank_send.at[k],
            recv_sem=bank_recv.at[k],
            device_id={"patch": lax.rem(me + k, patches)},
            device_id_type=MESH,
        )
        copy.start()
        bank_copies.append(copy)

    local_row = lax.broadcasted_iota(jnp.int32, (rows, LANES), 0)
    wave_rows = (local_row // BLOCK * (freqs * zbins) + f * zbins + z) * BLOCK + local_row % BLOCK
    lane = lax.broadcasted_iota(jnp.int32, (rows, LANES), 1)
    lower_edges = edges_ref[pl.ds(0, LANES)].reshape(1, LANES)
    upper_edges = edges_ref[pl.ds(1, LANES)].reshape(1, LANES)
    low = lower_edges[:, :1]
    reach = edge_reach(upper_edges, wave_rows)

    def band_sums(at, pairs):
        height = heights[at]
        index = (jnp.clip(reach - at * LANES, 1, LANES) - 1)[:height]
        inside = (reach > at * LANES)[:height]
        wave_cols = lane + at * LANES
        scale = (wave_rows * wave_rows + wave_cols * wave_cols >= low * low).astype(jnp.float32)
        if at == 0:
            scale = scale * jnp.where(lane == 0, 0.5, 1.0)
        scale = scale[:height]
        part = pl.ds(0, height)
        for (d1, b1), (d2, b2) in pairs:
            cross = None
            for c in range(4):
                term = modes[d1, at, b1, c, part, :].astype(jnp.float32) * modes[d2, at, b2, c, part, :].astype(
                    jnp.float32
                )
                cross = term if cross is None else cross + term
            cross = cross * scale
            upper = cross.astype(jnp.bfloat16)
            lower = (cross - upper.astype(jnp.float32)).astype(jnp.bfloat16)
            sums = jnp.dot(
                jnp.concatenate([upper, lower], axis=1), prefix_ref[...], preferred_element_type=jnp.float32
            )
            taken = jnp.where(inside, jnp.take_along_axis(sums, index, axis=1), 0.0)
            g1 = lax.rem(z + zbins - d1, zbins) * bins + b1
            g2 = lax.rem(z + zbins - d2, zbins) * bins + b2
            first, second = jnp.minimum(g1, g2), jnp.maximum(g1, g2)
            number = first * bins_total - first * (first - 1) // 2 + second - first
            spot = number // pair_share
            line = pl.ds(number - spot * pair_share, 1)
            discs[spot, line, :] += jnp.sum(taken, axis=0, keepdims=True)

    done = [(0, b) for b in range(bins)]
    for at in range(blocks):
        band_sums(at, [(done[i], done[j]) for i in range(bins) for j in range(i, bins)])

    counts = jnp.zeros((1, LANES), jnp.int32)
    for start in range(0, half, LANES):
        every = start + lax.broadcasted_iota(jnp.int32, (LANES, LANES), 0)
        inner = jnp.maximum(2 * edge_reach(lower_edges, every) - 1, 0)
        outer = jnp.maximum(2 * edge_reach(upper_edges, every) - 1, 0)
        counts = counts + jnp.sum(outer - inner, axis=0, keepdims=True)

    for d in range(1, zbins):
        new = [(d, b) for b in range(bins)]
        pairs = [(a, c) for a in done for c in new]
        pairs += [(new[i], new[j]) for i in range(bins) for j in range(i, bins)]
        for at in range(blocks):
            modes_copies[d, at].wait_recv()
            band_sums(at, pairs)
        done += new
    loads[3].wait()

    copies = []
    for n, (dz, df) in enumerate(group):
        target = lax.rem(z + dz, zbins)
        copy = pltpu.make_async_remote_copy(
            src_ref=discs.at[target],
            dst_ref=shares.at[n],
            send_sem=share_ssem.at[n],
            recv_sem=share_rsem.at[n],
            device_id={"zbin": target, "freq": lax.rem(f + df, freqs)},
            device_id_type=MESH,
        )
        copy.start()
        copies.append(copy)
    total = discs[z]
    for n, copy in enumerate(copies):
        copy.wait_recv()
        total = total + shares[n]
    for copy in bank_copies:
        copy.wait_recv()

    shifted = pltpu.roll(total, 1, 1)
    shifted = jnp.where(lax.broadcasted_iota(jnp.int32, total.shape, 1) == 0, 0.0, shifted)
    pseudo = (total - shifted) / (counts.astype(jnp.float32) * float(length * length))
    kind = class_ref[me]
    holder = kind // bank.shape[1]
    matrix = bank[lax.rem(me - holder + patches, patches), kind - holder * bank.shape[1]]
    result = lax.dot_general(
        pseudo,
        matrix,
        (((1,), (1,)), ((), ())),
        precision=lax.Precision.HIGHEST,
        preferred_element_type=jnp.float32,
    )
    for q in range(pair_share):
        out_ref[q] = result[q : q + 1]

    for copy in strip_copies + bank_copies + list(cols_copies.values()) + list(modes_copies.values()) + copies:
        copy.wait_send()


def per_device(density_maps, margin_src, margin_row, margin_count, class_id, coupling_bank, band_edges):
    _, bins, length, columns = density_maps.shape
    half = length // 2
    freqs = lax.axis_size("freq")
    zbins = lax.axis_size("zbin")
    patches = lax.axis_size("patch")
    rows = half // freqs // zbins
    bins_total = bins * zbins
    pair_share = bins_total * (bins_total + 1) // 2 // zbins
    padded = -(-pair_share // 8) * 8
    group = zbins * freqs - 1
    blocks = half // LANES

    profile = taper_profile(length, APOD)
    ramp = np.concatenate([profile[:APOD], profile[length - APOD :]])[:, None]
    cos_np, sin_np = fourier_tables(length)
    minus_sin = (-sin_np.astype(np.float32)).astype(ml_dtypes.bfloat16)
    spot = np.arange(half)
    dealt = (spot % rows // BLOCK * (freqs * zbins) + spot // rows) * BLOCK + spot % BLOCK
    table = np.concatenate([cos_np[dealt], minus_sin[dealt]], axis=0)
    turn = np.stack(
        [
            np.concatenate([cos_np.T[:, at : at + LANES], sin_np.T[:, at : at + LANES]], axis=1)
            for at in range(0, half, LANES)
        ]
    )
    ones = np.triu(np.ones((LANES, LANES)))
    prefix = np.concatenate([ones, ones], axis=0).astype(ml_dtypes.bfloat16)

    smem = pl.BlockSpec(memory_space=pltpu.SMEM)
    vmem = pl.BlockSpec(memory_space=pltpu.VMEM)
    anywhere = pl.BlockSpec(memory_space=pl.ANY)
    dma = pltpu.SemaphoreType.DMA
    bf16, f32 = jnp.bfloat16, jnp.float32
    sizes = (patches, zbins, freqs)
    spectra = pl.pallas_call(
        lambda *refs: kernel(sizes, *refs),
        out_shape=jax.ShapeDtypeStruct((pair_share, 1, LANES), f32),
        in_specs=[smem] * 4 + [vmem] * 4 + [anywhere] * 4,
        out_specs=vmem,
        scratch_shapes=[
            pltpu.VMEM((bins, length, columns), bf16),
            pltpu.VMEM((length, length), bf16),
            pltpu.VMEM((blocks, length, 2 * LANES), bf16),
            pltpu.VMEM((bins, 4, W, columns), bf16),
            pltpu.VMEM((patches,) + coupling_bank.shape, f32),
            pltpu.VMEM((bins, length, columns), bf16),
            pltpu.VMEM((zbins, bins * 2 * rows, columns), bf16),
            pltpu.VMEM((zbins, bins * 2 * rows, columns), bf16),
            pltpu.VMEM((zbins, bins * 2 * rows, columns), bf16),
            pltpu.VMEM((zbins, blocks, bins, 4, rows, LANES), bf16),
            pltpu.VMEM((zbins, blocks, bins, 4, rows, LANES), bf16),
            pltpu.VMEM((zbins, padded, LANES), f32),
            pltpu.VMEM((group, padded, LANES), f32),
            dma((4,)), dma((4,)), dma((4,)), dma((patches,)), dma((patches,)), dma((zbins,)), dma((zbins,)),
            dma((zbins, blocks)), dma((zbins, blocks)), dma((group,)), dma((group,)),
        ],
        compiler_params=pltpu.CompilerParams(
            collective_id=0, has_side_effects=True, vmem_limit_bytes=56 * 1024 * 1024
        ),
        name="spectra",
    )(
        margin_src, margin_row, margin_count, class_id, band_edges, jnp.asarray(ramp),
        jnp.asarray(profile)[None, :], jnp.asarray(prefix),
        density_maps, coupling_bank, jnp.asarray(table), jnp.asarray(turn),
    )
    return jnp.transpose(spectra, (1, 0, 2))


def solution(mesh):
    in_specs = (
        P(("groups", "patch"), "zbin", None, "freq"),
        P("groups", None),
        P("groups", None),
        P("groups"),
        P("groups"),
        P("patch", None, None),
        P(),
    )
    out_specs = P(("groups", "patch"), "zbin", None)
    return jax.shard_map(
        per_device, mesh=mesh, in_specs=in_specs, out_specs=out_specs, check_vma=False
    )
```

```python
import math

import jax
import jax.numpy as jnp
import ml_dtypes
import numpy as np
from jax import lax
from jax.experimental import pallas as pl
from jax.experimental.pallas import tpu as pltpu
from jax.sharding import PartitionSpec as P

W = 32
BLOCK = 16
APOD = 64
LANES = 128
MESH = pl.DeviceIdType.MESH


def taper_profile(length, ramp_width):
    position = np.arange(length)
    distance = np.minimum(position, length - 1 - position)
    ramped = 0.5 - 0.5 * np.cos(math.pi * (distance + 0.5) / ramp_width)
    return np.where(distance < ramp_width, ramped, 1.0).astype(np.float32)


def fourier_tables(length):
    half = length // 2
    phases = np.arange(half)[:, None] * np.arange(length)[None, :] % length
    angles = phases * (2.0 * math.pi / length)
    return (
        np.cos(angles).astype(np.float32).astype(ml_dtypes.bfloat16),
        np.sin(angles).astype(np.float32).astype(ml_dtypes.bfloat16),
    )


def edge_reach(edges, wave_rows):
    room = edges * edges - wave_rows * wave_rows
    reach = jnp.sqrt(jnp.maximum(room, 0).astype(jnp.float32)).astype(jnp.int32) - 1
    for _ in range(3):
        reach = reach + (reach * reach < room).astype(jnp.int32)
    return jnp.where(room > 0, reach, 0)


def kernel(
    sizes,
    src_ref, row_ref, count_ref, class_ref, edges_ref, ramp_ref, col_taper_ref, prefix_ref,
    maps_hbm, bank_hbm, table_hbm, turn_hbm,
    out_ref,
    maps, table, turn, strips, bank, tapered,
    waiting, strip_table, strip_rows, cols_send, cols_own, cols_recv, modes_send, modes, discs, shares,
    load_sem, strip_send, strip_recv, bank_send, bank_recv, cols_ssem, cols_rsem,
    modes_ssem, modes_rsem, share_ssem, share_rsem,
):
    patches, zbins, freqs = sizes
    bins, length, columns = maps.shape
    half = length // 2
    rows_freq = half // freqs
    rows = rows_freq // zbins
    bins_total = bins * zbins
    pair_total = bins_total * (bins_total + 1) // 2
    pair_share = pair_total // zbins
    me = lax.axis_index("patch")
    z = lax.axis_index("zbin")
    f = lax.axis_index("freq")
    other = 1 - f
    right, left = lax.rem(me + 1, patches), lax.rem(me + patches - 1, patches)

    loads = [
        pltpu.make_async_copy(maps_hbm.at[0], maps, load_sem.at[0]),
        pltpu.make_async_copy(table_hbm, table, load_sem.at[1]),
        pltpu.make_async_copy(turn_hbm, turn, load_sem.at[2]),
        pltpu.make_async_copy(bank_hbm, bank.at[0], load_sem.at[3]),
    ]
    for load in loads:
        load.start()

    group = [(dz, df) for dz in range(zbins) for df in range(freqs) if (dz, df) != (0, 0)]
    barrier = pltpu.get_barrier_semaphore()
    for k in range(1, patches):
        pl.semaphore_signal(barrier, inc=1, device_id={"patch": lax.rem(me + k, patches)}, device_id_type=MESH)
    for dz, df in group:
        pl.semaphore_signal(
            barrier,
            inc=1,
            device_id={"zbin": lax.rem(z + dz, zbins), "freq": lax.rem(f + df, freqs)},
            device_id_type=MESH,
        )
    pl.semaphore_wait(barrier, patches - 1 + len(group))

    strip_copies = []
    for side, target in ((0, right), (1, left)):
        for s, at in ((0, 0), (1, length - W)):
            slot = side * 2 + s
            copy = pltpu.make_async_remote_copy(
                src_ref=maps_hbm.at[0, :, pl.ds(at, W), :],
                dst_ref=strips.at[:, slot],
                send_sem=strip_send.at[slot],
                recv_sem=strip_recv.at[slot],
                device_id={"patch": target},
                device_id_type=MESH,
            )
            copy.start()
            strip_copies.append(copy)

    discs[...] = jnp.zeros_like(discs)
    entries = []
    for k in range(src_ref.shape[1]):
        source = src_ref[me, k]
        side = jnp.where(lax.shift_right_logical(source, 1) == left, 0, 1)
        entries.append((side * 2 + (source & 1), k < count_ref[me], row_ref[me, k]))
    def entry_rows(shape, axis):
        place = lax.broadcasted_iota(jnp.int32, shape, axis)
        rows_at = jnp.full(shape, -1, jnp.int32)
        for k, (_, live, row) in enumerate(entries):
            rows_at = jnp.where((place // W == k) & live, row + place % W, rows_at)
        return rows_at

    slots = len(entries) * W
    loads[0].wait()
    col_taper = col_taper_ref[:, pl.ds(pl.multiple_of(f * columns, columns), columns)]
    bounds = [0, APOD] + list(range(4 * APOD, length - APOD, 4 * APOD)) + [length - APOD, length]
    for start, stop in zip(bounds[:-1], bounds[1:]):
        for b in range(bins):
            image = maps[b, pl.ds(start, stop - start), :].astype(jnp.float32)
            if start == 0:
                image = image * ramp_ref[pl.ds(0, APOD), :]
            if stop == length:
                image = image * ramp_ref[pl.ds(APOD, APOD), :]
            tapered[b, pl.ds(start, stop - start), :] = (image * col_taper).astype(jnp.bfloat16)

    order = list(range(1, zbins)) + [0]
    blocks = half // LANES
    spread = freqs * zbins * BLOCK
    heights = [
        BLOCK * sum((at * LANES) ** 2 + (t * spread) ** 2 < (half - 1) ** 2 for t in range(rows // BLOCK))
        for at in range(blocks)
    ]
    loads[1].wait()

    def rows_of(ref, half_index, d):
        base = half_index * rows_freq + lax.rem(z + d, zbins) * rows
        return jnp.concatenate(
            [
                ref[pl.ds(pl.multiple_of(base, rows), rows), :],
                ref[pl.ds(pl.multiple_of(half + base, rows), rows), :],
            ],
            axis=0,
        )

    def base_product(half_index, d, b):
        return jnp.dot(rows_of(table, half_index, d), tapered[b], preferred_element_type=jnp.float32)

    def strip_product(half_index, d, b):
        return jnp.dot(rows_of(strip_table, half_index, d), strip_rows[b], preferred_element_type=jnp.float32)

    early = order[0]
    for part, half_index in enumerate((other, f)):
        for b in range(bins):
            waiting[part, b] = base_product(half_index, early, b)
    pixel = lax.broadcasted_iota(jnp.int32, (length, slots), 0)
    pick = (pixel == entry_rows((1, slots), 1)).astype(jnp.float32).astype(jnp.bfloat16)
    strip_table[...] = jnp.dot(table[...], pick, preferred_element_type=jnp.float32).astype(jnp.bfloat16)
    across = lax.broadcasted_iota(jnp.int32, (slots, length), 1)
    found = across == entry_rows((slots, 1), 0)
    strip_taper = jnp.sum(jnp.where(found, col_taper_ref[...], 0.0), axis=1, keepdims=True)

    for copy in strip_copies:
        copy.wait_recv()
    for b in range(bins):
        for k, (slot, _, _) in enumerate(entries):
            strip = strips[b, slot].astype(jnp.float32) * strip_taper[k * W : (k + 1) * W]
            strip_rows[b, pl.ds(k * W, W), :] = (strip * col_taper).astype(jnp.bfloat16)

    def second_transform(d, b, at, target):
        own = pl.ds(pl.multiple_of(f * columns, columns), columns)
        far = pl.ds(pl.multiple_of(other * columns, columns), columns)
        both = jnp.dot(cols_own[d, b], turn[at, own, :], preferred_element_type=jnp.float32) + jnp.dot(
            cols_recv[d, b], turn[at, far, :], preferred_element_type=jnp.float32
        )
        real_cos, real_sin = both[:rows, :LANES], both[:rows, LANES:]
        imag_cos, imag_sin = both[rows:, :LANES], both[rows:, LANES:]
        target[d, at, b, 0] = (real_cos + imag_sin).astype(jnp.bfloat16)
        target[d, at, b, 1] = (real_cos - imag_sin).astype(jnp.bfloat16)
        target[d, at, b, 2] = (imag_cos - real_sin).astype(jnp.bfloat16)
        target[d, at, b, 3] = (imag_cos + real_sin).astype(jnp.bfloat16)

    cols_copies, modes_copies = {}, {}

    def send_cols(d, b):
        copy = pltpu.make_async_remote_copy(
            src_ref=cols_send.at[d, b],
            dst_ref=cols_recv.at[d, b],
            send_sem=cols_ssem.at[d, b],
            recv_sem=cols_rsem.at[d, b],
            device_id={"freq": other},
            device_id_type=MESH,
        )
        copy.start()
        cols_copies[d, b] = copy

    for d in order:
        for b in range(bins):
            base = waiting[0, b] if d == early else base_product(other, d, b)
            cols_send[d, b] = (base + strip_product(other, d, b)).astype(jnp.bfloat16)
            send_cols(d, b)
        for b in range(bins):
            base = waiting[1, b] if d == early else base_product(f, d, b)
            cols_own[d, b] = (base + strip_product(f, d, b)).astype(jnp.bfloat16)
        if d == early:
            loads[2].wait()
        for b in range(bins):
            cols_copies[d, b].wait_recv()
            for at in range(blocks):
                second_transform(d, b, at, modes_send if d else modes)
                if d:
                    part = pl.ds(0, heights[at])
                    copy = pltpu.make_async_remote_copy(
                        src_ref=modes_send.at[d, at, b, :, part, :],
                        dst_ref=modes.at[d, at, b, :, part, :],
                        send_sem=modes_ssem.at[d, b * blocks + at],
                        recv_sem=modes_rsem.at[d, b * blocks + at],
                        device_id={"zbin": lax.rem(z + d, zbins)},
                        device_id_type=MESH,
                    )
                    copy.start()
                    modes_copies[d, b, at] = copy

    bank_copies = []
    for k in range(1, patches):
        copy = pltpu.make_async_remote_copy(
            src_ref=bank_hbm,
            dst_ref=bank.at[k],
            send_sem=bank_send.at[k],
            recv_sem=bank_recv.at[k],
            device_id={"patch": lax.rem(me + k, patches)},
            device_id_type=MESH,
        )
        copy.start()
        bank_copies.append(copy)

    local_row = lax.broadcasted_iota(jnp.int32, (rows, LANES), 0)
    wave_rows = (local_row // BLOCK * (freqs * zbins) + f * zbins + z) * BLOCK + local_row % BLOCK
    lane = lax.broadcasted_iota(jnp.int32, (rows, LANES), 1)
    lower_edges = edges_ref[pl.ds(0, LANES)].reshape(1, LANES)
    upper_edges = edges_ref[pl.ds(1, LANES)].reshape(1, LANES)
    low = lower_edges[:, :1]
    reach = edge_reach(upper_edges, wave_rows)

    def band_sums(at, pairs):
        height = heights[at]
        index = (jnp.clip(reach - at * LANES, 1, LANES) - 1)[:height]
        inside = (reach > at * LANES)[:height]
        wave_cols = lane + at * LANES
        scale = (wave_rows * wave_rows + wave_cols * wave_cols >= low * low).astype(jnp.float32)
        if at == 0:
            scale = scale * jnp.where(lane == 0, 0.5, 1.0)
        scale = scale[:height]
        part = pl.ds(0, height)
        for (d1, b1), (d2, b2) in pairs:
            cross = None
            for c in range(4):
                term = modes[d1, at, b1, c, part, :].astype(jnp.float32) * modes[d2, at, b2, c, part, :].astype(
                    jnp.float32
                )
                cross = term if cross is None else cross + term
            cross = cross * scale
            upper = cross.astype(jnp.bfloat16)
            lower = (cross - upper.astype(jnp.float32)).astype(jnp.bfloat16)
            sums = jnp.dot(
                jnp.concatenate([upper, lower], axis=1), prefix_ref[...], preferred_element_type=jnp.float32
            )
            taken = jnp.where(inside, jnp.take_along_axis(sums, index, axis=1), 0.0)
            g1 = lax.rem(z + zbins - d1, zbins) * bins + b1
            g2 = lax.rem(z + zbins - d2, zbins) * bins + b2
            first, second = jnp.minimum(g1, g2), jnp.maximum(g1, g2)
            number = first * bins_total - first * (first - 1) // 2 + second - first
            spot = number // pair_share
            line = pl.ds(number - spot * pair_share, 1)
            discs[spot, line, :] += jnp.sum(taken, axis=0, keepdims=True)

    done = [(0, b) for b in range(bins)]
    for at in range(blocks):
        band_sums(at, [(done[i], done[j]) for i in range(bins) for j in range(i, bins)])

    counts = jnp.zeros((1, LANES), jnp.int32)
    for start in range(0, half, LANES):
        every = start + lax.broadcasted_iota(jnp.int32, (LANES, LANES), 0)
        inner = jnp.maximum(2 * edge_reach(lower_edges, every) - 1, 0)
        outer = jnp.maximum(2 * edge_reach(upper_edges, every) - 1, 0)
        counts = counts + jnp.sum(outer - inner, axis=0, keepdims=True)

    for d in range(1, zbins):
        for b in range(bins):
            done.append((d, b))
            for at in range(blocks):
                modes_copies[d, b, at].wait_recv()
                band_sums(at, [(old, (d, b)) for old in done])
    loads[3].wait()

    copies = []
    for n, (dz, df) in enumerate(group):
        target = lax.rem(z + dz, zbins)
        copy = pltpu.make_async_remote_copy(
            src_ref=discs.at[target],
            dst_ref=shares.at[n],
            send_sem=share_ssem.at[n],
            recv_sem=share_rsem.at[n],
            device_id={"zbin": target, "freq": lax.rem(f + df, freqs)},
            device_id_type=MESH,
        )
        copy.start()
        copies.append(copy)
    total = discs[z]
    for n, copy in enumerate(copies):
        copy.wait_recv()
        total = total + shares[n]
    for copy in bank_copies:
        copy.wait_recv()

    shifted = pltpu.roll(total, 1, 1)
    shifted = jnp.where(lax.broadcasted_iota(jnp.int32, total.shape, 1) == 0, 0.0, shifted)
    pseudo = (total - shifted) / (counts.astype(jnp.float32) * float(length * length))
    kind = class_ref[me]
    holder = kind // bank.shape[1]
    matrix = bank[lax.rem(me - holder + patches, patches), kind - holder * bank.shape[1]]
    result = lax.dot_general(
        pseudo,
        matrix,
        (((1,), (1,)), ((), ())),
        precision=lax.Precision.HIGHEST,
        preferred_element_type=jnp.float32,
    )
    for q in range(pair_share):
        out_ref[q] = result[q : q + 1]

    for copy in strip_copies + bank_copies + list(cols_copies.values()) + list(modes_copies.values()) + copies:
        copy.wait_send()


def per_device(density_maps, margin_src, margin_row, margin_count, class_id, coupling_bank, band_edges):
    _, bins, length, columns = density_maps.shape
    half = length // 2
    freqs = lax.axis_size("freq")
    zbins = lax.axis_size("zbin")
    patches = lax.axis_size("patch")
    rows = half // freqs // zbins
    bins_total = bins * zbins
    pair_share = bins_total * (bins_total + 1) // 2 // zbins
    padded = -(-pair_share // 8) * 8
    group = zbins * freqs - 1
    slots = margin_src.shape[1] * W
    blocks = half // LANES

    profile = taper_profile(length, APOD)
    ramp = np.concatenate([profile[:APOD], profile[length - APOD :]])[:, None]
    cos_np, sin_np = fourier_tables(length)
    minus_sin = (-sin_np.astype(np.float32)).astype(ml_dtypes.bfloat16)
    spot = np.arange(half)
    dealt = (spot % rows // BLOCK * (freqs * zbins) + spot // rows) * BLOCK + spot % BLOCK
    table = np.concatenate([cos_np[dealt], minus_sin[dealt]], axis=0)
    turn = np.stack(
        [
            np.concatenate([cos_np.T[:, at : at + LANES], sin_np.T[:, at : at + LANES]], axis=1)
            for at in range(0, half, LANES)
        ]
    )
    ones = np.triu(np.ones((LANES, LANES)))
    prefix = np.concatenate([ones, ones], axis=0).astype(ml_dtypes.bfloat16)

    smem = pl.BlockSpec(memory_space=pltpu.SMEM)
    vmem = pl.BlockSpec(memory_space=pltpu.VMEM)
    anywhere = pl.BlockSpec(memory_space=pl.ANY)
    dma = pltpu.SemaphoreType.DMA
    bf16, f32 = jnp.bfloat16, jnp.float32
    sizes = (patches, zbins, freqs)
    spectra = pl.pallas_call(
        lambda *refs: kernel(sizes, *refs),
        out_shape=jax.ShapeDtypeStruct((pair_share, 1, LANES), f32),
        in_specs=[smem] * 4 + [vmem] * 4 + [anywhere] * 4,
        out_specs=vmem,
        scratch_shapes=[
            pltpu.VMEM((bins, length, columns), bf16),
            pltpu.VMEM((length, length), bf16),
            pltpu.VMEM((blocks, length, 2 * LANES), bf16),
            pltpu.VMEM((bins, 4, W, columns), bf16),
            pltpu.VMEM((patches,) + coupling_bank.shape, f32),
            pltpu.VMEM((bins, length, columns), bf16),
            pltpu.VMEM((2, bins, 2 * rows, columns), f32),
            pltpu.VMEM((length, slots), bf16),
            pltpu.VMEM((bins, slots, columns), bf16),
            pltpu.VMEM((zbins, bins, 2 * rows, columns), bf16),
            pltpu.VMEM((zbins, bins, 2 * rows, columns), bf16),
            pltpu.VMEM((zbins, bins, 2 * rows, columns), bf16),
            pltpu.VMEM((zbins, blocks, bins, 4, rows, LANES), bf16),
            pltpu.VMEM((zbins, blocks, bins, 4, rows, LANES), bf16),
            pltpu.VMEM((zbins, padded, LANES), f32),
            pltpu.VMEM((group, padded, LANES), f32),
            dma((4,)), dma((4,)), dma((4,)), dma((patches,)), dma((patches,)), dma((zbins, bins)), dma((zbins, bins)),
            dma((zbins, bins * blocks)), dma((zbins, bins * blocks)), dma((group,)), dma((group,)),
        ],
        compiler_params=pltpu.CompilerParams(
            collective_id=0, has_side_effects=True, vmem_limit_bytes=56 * 1024 * 1024
        ),
        name="spectra",
    )(
        margin_src, margin_row, margin_count, class_id, band_edges, jnp.asarray(ramp),
        jnp.asarray(profile)[None, :], jnp.asarray(prefix),
        density_maps, coupling_bank, jnp.asarray(table), jnp.asarray(turn),
    )
    return jnp.transpose(spectra, (1, 0, 2))


def solution(mesh):
    in_specs = (
        P(("groups", "patch"), "zbin", None, "freq"),
        P("groups", None),
        P("groups", None),
        P("groups"),
        P("groups"),
        P("patch", None, None),
        P(),
    )
    out_specs = P(("groups", "patch"), "zbin", None)
    return jax.shard_map(
        per_device, mesh=mesh, in_specs=in_specs, out_specs=out_specs, check_vma=False
    )
```

```python
import math

import jax
import jax.numpy as jnp
import ml_dtypes
import numpy as np
from jax import lax
from jax.experimental import pallas as pl
from jax.experimental.pallas import tpu as pltpu
from jax.sharding import PartitionSpec as P

W = 32
BLOCK = 16
APOD = 64
LANES = 128
MESH = pl.DeviceIdType.MESH


def taper_profile(length, ramp_width):
    position = np.arange(length)
    distance = np.minimum(position, length - 1 - position)
    ramped = 0.5 - 0.5 * np.cos(math.pi * (distance + 0.5) / ramp_width)
    return np.where(distance < ramp_width, ramped, 1.0).astype(np.float32)


def fourier_tables(length):
    half = length // 2
    phases = np.arange(half)[:, None] * np.arange(length)[None, :] % length
    angles = phases * (2.0 * math.pi / length)
    return (
        np.cos(angles).astype(np.float32).astype(ml_dtypes.bfloat16),
        np.sin(angles).astype(np.float32).astype(ml_dtypes.bfloat16),
    )


def edge_reach(edges, wave_rows):
    room = edges * edges - wave_rows * wave_rows
    reach = jnp.sqrt(jnp.maximum(room, 0).astype(jnp.float32)).astype(jnp.int32) - 1
    for _ in range(3):
        reach = reach + (reach * reach < room).astype(jnp.int32)
    return jnp.where(room > 0, reach, 0)


def kernel(
    sizes,
    src_ref, row_ref, count_ref, class_ref, edges_ref, ramp_ref, col_taper_ref, prefix_ref,
    maps_hbm, bank_hbm, table_hbm, turn_hbm,
    out_ref,
    maps, table, turn, strips, bank, tapered,
    waiting, strip_table, strip_rows, cols_send, cols_own, cols_recv, modes_send, modes, discs, shares,
    load_sem, strip_send, strip_recv, bank_send, bank_recv, cols_ssem, cols_rsem,
    modes_ssem, modes_rsem, share_ssem, share_rsem,
):
    patches, zbins, freqs = sizes
    bins, length, columns = maps.shape
    half = length // 2
    rows_freq = half // freqs
    rows = rows_freq // zbins
    bins_total = bins * zbins
    pair_total = bins_total * (bins_total + 1) // 2
    pair_share = pair_total // zbins
    me = lax.axis_index("patch")
    z = lax.axis_index("zbin")
    f = lax.axis_index("freq")
    other = 1 - f
    right, left = lax.rem(me + 1, patches), lax.rem(me + patches - 1, patches)

    loads = [
        pltpu.make_async_copy(table_hbm, table, load_sem.at[0]),
        pltpu.make_async_copy(turn_hbm, turn, load_sem.at[1]),
        pltpu.make_async_copy(bank_hbm, bank.at[0], load_sem.at[2]),
    ]
    map_loads = [pltpu.make_async_copy(maps_hbm.at[0, b], maps.at[b], load_sem.at[3 + b]) for b in range(bins)]
    for load in map_loads[:1] + loads[:1] + map_loads[1:] + loads[1:]:
        load.start()

    group = [(dz, df) for dz in range(zbins) for df in range(freqs) if (dz, df) != (0, 0)]
    barrier = pltpu.get_barrier_semaphore()
    for k in range(1, patches):
        pl.semaphore_signal(barrier, inc=1, device_id={"patch": lax.rem(me + k, patches)}, device_id_type=MESH)
    for dz, df in group:
        pl.semaphore_signal(
            barrier,
            inc=1,
            device_id={"zbin": lax.rem(z + dz, zbins), "freq": lax.rem(f + df, freqs)},
            device_id_type=MESH,
        )
    pl.semaphore_wait(barrier, patches - 1 + len(group))

    strip_copies = {b: [] for b in range(bins)}
    for b in range(bins):
        for side, target in ((0, right), (1, left)):
            for half_side, at in ((0, 0), (1, length - W)):
                slot = side * 2 + half_side
                copy = pltpu.make_async_remote_copy(
                    src_ref=maps_hbm.at[0, b, pl.ds(at, W), :],
                    dst_ref=strips[b].at[slot],
                    send_sem=strip_send.at[b, slot],
                    recv_sem=strip_recv.at[b, slot],
                    device_id={"patch": target},
                    device_id_type=MESH,
                )
                copy.start()
                strip_copies[b].append(copy)

    discs[...] = jnp.zeros_like(discs)
    entries = []
    for k in range(src_ref.shape[1]):
        source = src_ref[me, k]
        side = jnp.where(lax.shift_right_logical(source, 1) == left, 0, 1)
        entries.append((side * 2 + (source & 1), k < count_ref[me], row_ref[me, k]))
    def entry_rows(shape, axis):
        place = lax.broadcasted_iota(jnp.int32, shape, axis)
        rows_at = jnp.full(shape, -1, jnp.int32)
        for k, (_, live, row) in enumerate(entries):
            rows_at = jnp.where((place // W == k) & live, row + place % W, rows_at)
        return rows_at

    slots = len(entries) * W
    col_taper = col_taper_ref[:, pl.ds(pl.multiple_of(f * columns, columns), columns)]
    bounds = [0, APOD] + list(range(4 * APOD, length - APOD, 4 * APOD)) + [length - APOD, length]

    def taper(b):
        map_loads[b].wait()
        for start, stop in zip(bounds[:-1], bounds[1:]):
            image = maps[b, pl.ds(start, stop - start), :].astype(jnp.float32)
            if start == 0:
                image = image * ramp_ref[pl.ds(0, APOD), :]
            if stop == length:
                image = image * ramp_ref[pl.ds(APOD, APOD), :]
            tapered[b, pl.ds(start, stop - start), :] = (image * col_taper).astype(jnp.bfloat16)

    order = list(range(1, zbins)) + [0]
    blocks = half // LANES
    spread = freqs * zbins * BLOCK
    heights = [
        BLOCK * sum((at * LANES) ** 2 + (t * spread) ** 2 < (half - 1) ** 2 for t in range(rows // BLOCK))
        for at in range(blocks)
    ]
    def rows_of(ref, half_index, d):
        base = half_index * rows_freq + lax.rem(z + d, zbins) * rows
        return jnp.concatenate(
            [
                ref[pl.ds(pl.multiple_of(base, rows), rows), :],
                ref[pl.ds(pl.multiple_of(half + base, rows), rows), :],
            ],
            axis=0,
        )

    def base_product(half_index, d, b):
        return jnp.dot(rows_of(table, half_index, d), tapered[b], preferred_element_type=jnp.float32)

    def strip_product(half_index, d, b):
        return jnp.dot(rows_of(strip_table, half_index, d), strip_rows[b], preferred_element_type=jnp.float32)

    def prepare(b):
        taper(b)
        if b == 0:
            loads[0].wait()
        for part, half_index in enumerate((other, f)):
            waiting[part, b] = base_product(half_index, early, b)

    def take_strips(b):
        for copy in strip_copies[b]:
            copy.wait_recv()
        for k, (slot, _, _) in enumerate(entries):
            strip = strips[b][slot].astype(jnp.float32) * strip_taper[k * W : (k + 1) * W]
            strip_rows[b, pl.ds(k * W, W), :] = (strip * col_taper).astype(jnp.bfloat16)

    early = order[0]
    across = lax.broadcasted_iota(jnp.int32, (slots, length), 1)
    found = across == entry_rows((slots, 1), 0)
    strip_taper = jnp.sum(jnp.where(found, col_taper_ref[...], 0.0), axis=1, keepdims=True)
    prepare(0)
    pixel = lax.broadcasted_iota(jnp.int32, (length, slots), 0)
    pick = (pixel == entry_rows((1, slots), 1)).astype(jnp.float32).astype(jnp.bfloat16)
    strip_table[...] = jnp.dot(table[...], pick, preferred_element_type=jnp.float32).astype(jnp.bfloat16)

    def second_transform(d, b, at, target):
        own = pl.ds(pl.multiple_of(f * columns, columns), columns)
        far = pl.ds(pl.multiple_of(other * columns, columns), columns)
        both = jnp.dot(cols_own[d, b], turn[at, own, :], preferred_element_type=jnp.float32) + jnp.dot(
            cols_recv[d, b], turn[at, far, :], preferred_element_type=jnp.float32
        )
        real_cos, real_sin = both[:rows, :LANES], both[:rows, LANES:]
        imag_cos, imag_sin = both[rows:, :LANES], both[rows:, LANES:]
        target[d, at, b, 0] = (real_cos + imag_sin).astype(jnp.bfloat16)
        target[d, at, b, 1] = (real_cos - imag_sin).astype(jnp.bfloat16)
        target[d, at, b, 2] = (imag_cos - real_sin).astype(jnp.bfloat16)
        target[d, at, b, 3] = (imag_cos + real_sin).astype(jnp.bfloat16)

    cols_copies, modes_copies = {}, {}

    def send_cols(d, b):
        copy = pltpu.make_async_remote_copy(
            src_ref=cols_send.at[d, b],
            dst_ref=cols_recv.at[d, b],
            send_sem=cols_ssem.at[d, b],
            recv_sem=cols_rsem.at[d, b],
            device_id={"freq": other},
            device_id_type=MESH,
        )
        copy.start()
        cols_copies[d, b] = copy

    def exchange_cols(d, b):
        base = waiting[0, b] if d == early else base_product(other, d, b)
        cols_send[d, b] = (base + strip_product(other, d, b)).astype(jnp.bfloat16)
        send_cols(d, b)
        base = waiting[1, b] if d == early else base_product(f, d, b)
        cols_own[d, b] = (base + strip_product(f, d, b)).astype(jnp.bfloat16)

    def make_modes(d, b):
        cols_copies[d, b].wait_recv()
        for at in range(blocks):
            second_transform(d, b, at, modes_send if d else modes)
            if d:
                part = pl.ds(0, heights[at])
                copy = pltpu.make_async_remote_copy(
                    src_ref=modes_send.at[d, at, b, :, part, :],
                    dst_ref=modes.at[d, at, b, :, part, :],
                    send_sem=modes_ssem.at[d, b * blocks + at],
                    recv_sem=modes_rsem.at[d, b * blocks + at],
                    device_id={"zbin": lax.rem(z + d, zbins)},
                    device_id_type=MESH,
                )
                copy.start()
                modes_copies[d, b, at] = copy

    for d in order:
        for b in range(bins):
            if d == early:
                take_strips(b)
            exchange_cols(d, b)
            if d == early and b + 1 < bins:
                prepare(b + 1)
            if d == early and b == 0:
                loads[1].wait()
            make_modes(d, b)

    bank_copies = []
    for k in range(1, patches):
        copy = pltpu.make_async_remote_copy(
            src_ref=bank_hbm,
            dst_ref=bank.at[k],
            send_sem=bank_send.at[k],
            recv_sem=bank_recv.at[k],
            device_id={"patch": lax.rem(me + k, patches)},
            device_id_type=MESH,
        )
        copy.start()
        bank_copies.append(copy)

    local_row = lax.broadcasted_iota(jnp.int32, (rows, LANES), 0)
    wave_rows = (local_row // BLOCK * (freqs * zbins) + f * zbins + z) * BLOCK + local_row % BLOCK
    lane = lax.broadcasted_iota(jnp.int32, (rows, LANES), 1)
    lower_edges = edges_ref[pl.ds(0, LANES)].reshape(1, LANES)
    upper_edges = edges_ref[pl.ds(1, LANES)].reshape(1, LANES)
    low = lower_edges[:, :1]
    reach = edge_reach(upper_edges, wave_rows)

    def band_sums(at, pairs):
        height = heights[at]
        index = (jnp.clip(reach - at * LANES, 1, LANES) - 1)[:height]
        inside = (reach > at * LANES)[:height]
        wave_cols = lane + at * LANES
        scale = (wave_rows * wave_rows + wave_cols * wave_cols >= low * low).astype(jnp.float32)
        if at == 0:
            scale = scale * jnp.where(lane == 0, 0.5, 1.0)
        scale = scale[:height]
        part = pl.ds(0, height)
        for (d1, b1), (d2, b2) in pairs:
            cross = None
            for c in range(4):
                term = modes[d1, at, b1, c, part, :].astype(jnp.float32) * modes[d2, at, b2, c, part, :].astype(
                    jnp.float32
                )
                cross = term if cross is None else cross + term
            cross = cross * scale
            upper = cross.astype(jnp.bfloat16)
            lower = (cross - upper.astype(jnp.float32)).astype(jnp.bfloat16)
            sums = jnp.dot(
                jnp.concatenate([upper, lower], axis=1), prefix_ref[...], preferred_element_type=jnp.float32
            )
            taken = jnp.where(inside, jnp.take_along_axis(sums, index, axis=1), 0.0)
            g1 = lax.rem(z + zbins - d1, zbins) * bins + b1
            g2 = lax.rem(z + zbins - d2, zbins) * bins + b2
            first, second = jnp.minimum(g1, g2), jnp.maximum(g1, g2)
            number = first * bins_total - first * (first - 1) // 2 + second - first
            spot = number // pair_share
            line = pl.ds(number - spot * pair_share, 1)
            discs[spot, line, :] += jnp.sum(taken, axis=0, keepdims=True)

    done = [(0, b) for b in range(bins)]
    for at in range(blocks):
        band_sums(at, [(done[i], done[j]) for i in range(bins) for j in range(i, bins)])

    counts = jnp.zeros((1, LANES), jnp.int32)
    for start in range(0, half, LANES):
        every = start + lax.broadcasted_iota(jnp.int32, (LANES, LANES), 0)
        inner = jnp.maximum(2 * edge_reach(lower_edges, every) - 1, 0)
        outer = jnp.maximum(2 * edge_reach(upper_edges, every) - 1, 0)
        counts = counts + jnp.sum(outer - inner, axis=0, keepdims=True)

    for d in range(1, zbins):
        for b in range(bins):
            done.append((d, b))
            for at in range(blocks):
                modes_copies[d, b, at].wait_recv()
                band_sums(at, [(old, (d, b)) for old in done])
    loads[2].wait()

    copies = []
    for n, (dz, df) in enumerate(group):
        target = lax.rem(z + dz, zbins)
        copy = pltpu.make_async_remote_copy(
            src_ref=discs.at[target],
            dst_ref=shares.at[n],
            send_sem=share_ssem.at[n],
            recv_sem=share_rsem.at[n],
            device_id={"zbin": target, "freq": lax.rem(f + df, freqs)},
            device_id_type=MESH,
        )
        copy.start()
        copies.append(copy)
    total = discs[z]
    for n, copy in enumerate(copies):
        copy.wait_recv()
        total = total + shares[n]
    for copy in bank_copies:
        copy.wait_recv()

    shifted = pltpu.roll(total, 1, 1)
    shifted = jnp.where(lax.broadcasted_iota(jnp.int32, total.shape, 1) == 0, 0.0, shifted)
    pseudo = (total - shifted) / (counts.astype(jnp.float32) * float(length * length))
    kind = class_ref[me]
    holder = kind // bank.shape[1]
    matrix = bank[lax.rem(me - holder + patches, patches), kind - holder * bank.shape[1]]
    result = lax.dot_general(
        pseudo,
        matrix,
        (((1,), (1,)), ((), ())),
        precision=lax.Precision.HIGHEST,
        preferred_element_type=jnp.float32,
    )
    for q in range(pair_share):
        out_ref[q] = result[q : q + 1]

    for copy in sum(strip_copies.values(), []) + bank_copies + list(cols_copies.values()) + list(modes_copies.values()) + copies:
        copy.wait_send()


def per_device(density_maps, margin_src, margin_row, margin_count, class_id, coupling_bank, band_edges):
    _, bins, length, columns = density_maps.shape
    half = length // 2
    freqs = lax.axis_size("freq")
    zbins = lax.axis_size("zbin")
    patches = lax.axis_size("patch")
    rows = half // freqs // zbins
    bins_total = bins * zbins
    pair_share = bins_total * (bins_total + 1) // 2 // zbins
    padded = -(-pair_share // 8) * 8
    group = zbins * freqs - 1
    slots = margin_src.shape[1] * W
    blocks = half // LANES

    profile = taper_profile(length, APOD)
    ramp = np.concatenate([profile[:APOD], profile[length - APOD :]])[:, None]
    cos_np, sin_np = fourier_tables(length)
    minus_sin = (-sin_np.astype(np.float32)).astype(ml_dtypes.bfloat16)
    spot = np.arange(half)
    dealt = (spot % rows // BLOCK * (freqs * zbins) + spot // rows) * BLOCK + spot % BLOCK
    table = np.concatenate([cos_np[dealt], minus_sin[dealt]], axis=0)
    turn = np.stack(
        [
            np.concatenate([cos_np.T[:, at : at + LANES], sin_np.T[:, at : at + LANES]], axis=1)
            for at in range(0, half, LANES)
        ]
    )
    ones = np.triu(np.ones((LANES, LANES)))
    prefix = np.concatenate([ones, ones], axis=0).astype(ml_dtypes.bfloat16)

    smem = pl.BlockSpec(memory_space=pltpu.SMEM)
    vmem = pl.BlockSpec(memory_space=pltpu.VMEM)
    anywhere = pl.BlockSpec(memory_space=pl.ANY)
    dma = pltpu.SemaphoreType.DMA
    bf16, f32 = jnp.bfloat16, jnp.float32
    sizes = (patches, zbins, freqs)
    spectra = pl.pallas_call(
        lambda *refs: kernel(sizes, *refs),
        out_shape=jax.ShapeDtypeStruct((pair_share, 1, LANES), f32),
        in_specs=[smem] * 4 + [vmem] * 4 + [anywhere] * 4,
        out_specs=vmem,
        scratch_shapes=[
            pltpu.VMEM((bins, length, columns), bf16),
            pltpu.VMEM((length, length), bf16),
            pltpu.VMEM((blocks, length, 2 * LANES), bf16),
            [pltpu.VMEM((4, W, columns), bf16)] * bins,
            pltpu.VMEM((patches,) + coupling_bank.shape, f32),
            pltpu.VMEM((bins, length, columns), bf16),
            pltpu.VMEM((2, bins, 2 * rows, columns), f32),
            pltpu.VMEM((length, slots), bf16),
            pltpu.VMEM((bins, slots, columns), bf16),
            pltpu.VMEM((zbins, bins, 2 * rows, columns), bf16),
            pltpu.VMEM((zbins, bins, 2 * rows, columns), bf16),
            pltpu.VMEM((zbins, bins, 2 * rows, columns), bf16),
            pltpu.VMEM((zbins, blocks, bins, 4, rows, LANES), bf16),
            pltpu.VMEM((zbins, blocks, bins, 4, rows, LANES), bf16),
            pltpu.VMEM((zbins, padded, LANES), f32),
            pltpu.VMEM((group, padded, LANES), f32),
            dma((3 + bins,)), dma((bins, 4)), dma((bins, 4)), dma((patches,)), dma((patches,)), dma((zbins, bins)), dma((zbins, bins)),
            dma((zbins, bins * blocks)), dma((zbins, bins * blocks)), dma((group,)), dma((group,)),
        ],
        compiler_params=pltpu.CompilerParams(
            collective_id=0, has_side_effects=True, vmem_limit_bytes=56 * 1024 * 1024
        ),
        name="spectra",
    )(
        margin_src, margin_row, margin_count, class_id, band_edges, jnp.asarray(ramp),
        jnp.asarray(profile)[None, :], jnp.asarray(prefix),
        density_maps, coupling_bank, jnp.asarray(table), jnp.asarray(turn),
    )
    return jnp.transpose(spectra, (1, 0, 2))


def solution(mesh):
    in_specs = (
        P(("groups", "patch"), "zbin", None, "freq"),
        P("groups", None),
        P("groups", None),
        P("groups"),
        P("groups"),
        P("patch", None, None),
        P(),
    )
    out_specs = P(("groups", "patch"), "zbin", None)
    return jax.shard_map(
        per_device, mesh=mesh, in_specs=in_specs, out_specs=out_specs, check_vma=False
    )
```

```python
import math

import jax
import jax.numpy as jnp
import ml_dtypes
import numpy as np
from jax import lax
from jax.experimental import pallas as pl
from jax.experimental.pallas import tpu as pltpu
from jax.sharding import PartitionSpec as P

W = 32
BLOCK = 16
APOD = 64
LANES = 128
MESH = pl.DeviceIdType.MESH


def taper_profile(length, ramp_width):
    position = np.arange(length)
    distance = np.minimum(position, length - 1 - position)
    ramped = 0.5 - 0.5 * np.cos(math.pi * (distance + 0.5) / ramp_width)
    return np.where(distance < ramp_width, ramped, 1.0).astype(np.float32)


def fourier_tables(length):
    half = length // 2
    phases = np.arange(half)[:, None] * np.arange(length)[None, :] % length
    angles = phases * (2.0 * math.pi / length)
    return (
        np.cos(angles).astype(np.float32).astype(ml_dtypes.bfloat16),
        np.sin(angles).astype(np.float32).astype(ml_dtypes.bfloat16),
    )


def edge_reach(edges, wave_rows):
    room = edges * edges - wave_rows * wave_rows
    reach = jnp.sqrt(jnp.maximum(room, 0).astype(jnp.float32)).astype(jnp.int32) - 1
    for _ in range(3):
        reach = reach + (reach * reach < room).astype(jnp.int32)
    return jnp.where(room > 0, reach, 0)


def kernel(
    sizes,
    src_ref, row_ref, count_ref, class_ref, edges_ref, ramp_ref, col_taper_ref, prefix_ref,
    maps_hbm, bank_hbm, table_hbm, turn_hbm,
    out_ref,
    maps, table, turn, strips, bank, tapered,
    waiting, strip_table, strip_rows, cols_send, cols_own, cols_recv, modes_send, modes, discs, shares,
    load_sem, strip_send, strip_recv, bank_send, bank_recv, cols_ssem, cols_rsem,
    modes_ssem, modes_rsem, share_ssem, share_rsem,
):
    patches, zbins, freqs = sizes
    bins, length, columns = maps.shape
    half = length // 2
    rows_freq = half // freqs
    rows = rows_freq // zbins
    bins_total = bins * zbins
    pair_total = bins_total * (bins_total + 1) // 2
    pair_share = pair_total // zbins
    me = lax.axis_index("patch")
    z = lax.axis_index("zbin")
    f = lax.axis_index("freq")
    other = 1 - f
    right, left = lax.rem(me + 1, patches), lax.rem(me + patches - 1, patches)

    loads = [
        pltpu.make_async_copy(table_hbm, table, load_sem.at[0]),
        pltpu.make_async_copy(turn_hbm, turn, load_sem.at[1]),
        pltpu.make_async_copy(bank_hbm, bank.at[0], load_sem.at[2]),
    ]
    map_loads = [pltpu.make_async_copy(maps_hbm.at[0, b], maps.at[b], load_sem.at[3 + b]) for b in range(bins)]
    for load in map_loads[:1] + loads[:1] + map_loads[1:] + loads[1:]:
        load.start()

    group = [(dz, df) for dz in range(zbins) for df in range(freqs) if (dz, df) != (0, 0)]
    barrier = pltpu.get_barrier_semaphore()
    for k in range(1, patches):
        pl.semaphore_signal(barrier, inc=1, device_id={"patch": lax.rem(me + k, patches)}, device_id_type=MESH)
    for dz, df in group:
        pl.semaphore_signal(
            barrier,
            inc=1,
            device_id={"zbin": lax.rem(z + dz, zbins), "freq": lax.rem(f + df, freqs)},
            device_id_type=MESH,
        )
    pl.semaphore_wait(barrier, patches - 1 + len(group))

    strip_copies = {b: [] for b in range(bins)}
    for b in range(bins):
        for side, target in ((0, right), (1, left)):
            for half_side, at in ((0, 0), (1, length - W)):
                slot = side * 2 + half_side
                copy = pltpu.make_async_remote_copy(
                    src_ref=maps_hbm.at[0, b, pl.ds(at, W), :],
                    dst_ref=strips[b].at[slot],
                    send_sem=strip_send.at[b, slot],
                    recv_sem=strip_recv.at[b, slot],
                    device_id={"patch": target},
                    device_id_type=MESH,
                )
                copy.start()
                strip_copies[b].append(copy)

    discs[...] = jnp.zeros_like(discs)
    entries = []
    for k in range(src_ref.shape[1]):
        source = src_ref[me, k]
        side = jnp.where(lax.shift_right_logical(source, 1) == left, 0, 1)
        entries.append((side * 2 + (source & 1), k < count_ref[me], row_ref[me, k]))
    def entry_rows(shape, axis):
        place = lax.broadcasted_iota(jnp.int32, shape, axis)
        rows_at = jnp.full(shape, -1, jnp.int32)
        for k, (_, live, row) in enumerate(entries):
            rows_at = jnp.where((place // W == k) & live, row + place % W, rows_at)
        return rows_at

    slots = len(entries) * W
    col_taper = col_taper_ref[:, pl.ds(pl.multiple_of(f * columns, columns), columns)]
    bounds = [0, APOD] + list(range(4 * APOD, length - APOD, 4 * APOD)) + [length - APOD, length]

    def taper(b):
        map_loads[b].wait()
        for start, stop in zip(bounds[:-1], bounds[1:]):
            image = maps[b, pl.ds(start, stop - start), :].astype(jnp.float32)
            if start == 0:
                image = image * ramp_ref[pl.ds(0, APOD), :]
            if stop == length:
                image = image * ramp_ref[pl.ds(APOD, APOD), :]
            tapered[b, pl.ds(start, stop - start), :] = (image * col_taper).astype(jnp.bfloat16)

    order = list(range(1, zbins)) + [0]
    blocks = half // LANES
    spread = freqs * zbins * BLOCK
    heights = [
        BLOCK * sum((at * LANES) ** 2 + (t * spread) ** 2 < (half - 1) ** 2 for t in range(rows // BLOCK))
        for at in range(blocks)
    ]
    def rows_of(ref, half_index, d):
        base = half_index * rows_freq + lax.rem(z + d, zbins) * rows
        return jnp.concatenate(
            [
                ref[pl.ds(pl.multiple_of(base, rows), rows), :],
                ref[pl.ds(pl.multiple_of(half + base, rows), rows), :],
            ],
            axis=0,
        )

    def base_product(half_index, d, b):
        return jnp.dot(rows_of(table, half_index, d), tapered[b], preferred_element_type=jnp.float32)

    def strip_product(half_index, d, b):
        return jnp.dot(rows_of(strip_table, half_index, d), strip_rows[b], preferred_element_type=jnp.float32)

    def prepare(b):
        taper(b)
        if b == 0:
            loads[0].wait()
        for part, half_index in enumerate((other, f)):
            waiting[part, b] = base_product(half_index, early, b)

    def take_strips(b):
        for copy in strip_copies[b]:
            copy.wait_recv()
        for k, (slot, _, _) in enumerate(entries):
            strip = strips[b][slot].astype(jnp.float32) * strip_taper[k * W : (k + 1) * W]
            strip_rows[b, pl.ds(k * W, W), :] = (strip * col_taper).astype(jnp.bfloat16)

    early = order[0]
    across = lax.broadcasted_iota(jnp.int32, (slots, length), 1)
    found = across == entry_rows((slots, 1), 0)
    strip_taper = jnp.sum(jnp.where(found, col_taper_ref[...], 0.0), axis=1, keepdims=True)
    prepare(0)
    pixel = lax.broadcasted_iota(jnp.int32, (length, slots), 0)
    pick = (pixel == entry_rows((1, slots), 1)).astype(jnp.float32).astype(jnp.bfloat16)
    strip_table[...] = jnp.dot(table[...], pick, preferred_element_type=jnp.float32).astype(jnp.bfloat16)

    def second_transform(d, b, at, target):
        own = pl.ds(pl.multiple_of(f * columns, columns), columns)
        far = pl.ds(pl.multiple_of(other * columns, columns), columns)
        both = jnp.dot(cols_own[d, b], turn[at, own, :], preferred_element_type=jnp.float32) + jnp.dot(
            cols_recv[d, b], turn[at, far, :], preferred_element_type=jnp.float32
        )
        real_cos, real_sin = both[:rows, :LANES], both[:rows, LANES:]
        imag_cos, imag_sin = both[rows:, :LANES], both[rows:, LANES:]
        target[d, at, b, 0] = (real_cos + imag_sin).astype(jnp.bfloat16)
        target[d, at, b, 1] = (real_cos - imag_sin).astype(jnp.bfloat16)
        target[d, at, b, 2] = (imag_cos - real_sin).astype(jnp.bfloat16)
        target[d, at, b, 3] = (imag_cos + real_sin).astype(jnp.bfloat16)

    cols_copies, modes_copies = {}, {}

    def send_cols(d, b):
        copy = pltpu.make_async_remote_copy(
            src_ref=cols_send.at[d, b],
            dst_ref=cols_recv.at[d, b],
            send_sem=cols_ssem.at[d, b],
            recv_sem=cols_rsem.at[d, b],
            device_id={"freq": other},
            device_id_type=MESH,
        )
        copy.start()
        cols_copies[d, b] = copy

    def exchange_cols(d, b):
        base = waiting[0, b] if d == early else base_product(other, d, b)
        cols_send[d, b] = (base + strip_product(other, d, b)).astype(jnp.bfloat16)
        send_cols(d, b)
        base = waiting[1, b] if d == early else base_product(f, d, b)
        cols_own[d, b] = (base + strip_product(f, d, b)).astype(jnp.bfloat16)

    def make_modes(d, b):
        cols_copies[d, b].wait_recv()
        for at in range(blocks):
            second_transform(d, b, at, modes_send if d else modes)
            if d:
                part = pl.ds(0, heights[at])
                copy = pltpu.make_async_remote_copy(
                    src_ref=modes_send.at[d, at, b, :, part, :],
                    dst_ref=modes.at[d, at, b, :, part, :],
                    send_sem=modes_ssem.at[d, b * blocks + at],
                    recv_sem=modes_rsem.at[d, b * blocks + at],
                    device_id={"zbin": lax.rem(z + d, zbins)},
                    device_id_type=MESH,
                )
                copy.start()
                modes_copies[d, b, at] = copy

    for d in order:
        for b in range(bins):
            if d == early:
                take_strips(b)
            exchange_cols(d, b)
            if d == early and b == 0:
                loads[1].wait()
            make_modes(d, b)
            if d == early and b + 1 < bins:
                prepare(b + 1)

    bank_copies = []
    for k in range(1, patches):
        copy = pltpu.make_async_remote_copy(
            src_ref=bank_hbm,
            dst_ref=bank.at[k],
            send_sem=bank_send.at[k],
            recv_sem=bank_recv.at[k],
            device_id={"patch": lax.rem(me + k, patches)},
            device_id_type=MESH,
        )
        copy.start()
        bank_copies.append(copy)

    local_row = lax.broadcasted_iota(jnp.int32, (rows, LANES), 0)
    wave_rows = (local_row // BLOCK * (freqs * zbins) + f * zbins + z) * BLOCK + local_row % BLOCK
    lane = lax.broadcasted_iota(jnp.int32, (rows, LANES), 1)
    lower_edges = edges_ref[pl.ds(0, LANES)].reshape(1, LANES)
    upper_edges = edges_ref[pl.ds(1, LANES)].reshape(1, LANES)
    low = lower_edges[:, :1]
    reach = edge_reach(upper_edges, wave_rows)

    def band_sums(at, pairs):
        height = heights[at]
        index = (jnp.clip(reach - at * LANES, 1, LANES) - 1)[:height]
        inside = (reach > at * LANES)[:height]
        wave_cols = lane + at * LANES
        scale = (wave_rows * wave_rows + wave_cols * wave_cols >= low * low).astype(jnp.float32)
        if at == 0:
            scale = scale * jnp.where(lane == 0, 0.5, 1.0)
        scale = scale[:height]
        part = pl.ds(0, height)
        for (d1, b1), (d2, b2) in pairs:
            cross = None
            for c in range(4):
                term = modes[d1, at, b1, c, part, :].astype(jnp.float32) * modes[d2, at, b2, c, part, :].astype(
                    jnp.float32
                )
                cross = term if cross is None else cross + term
            cross = cross * scale
            upper = cross.astype(jnp.bfloat16)
            lower = (cross - upper.astype(jnp.float32)).astype(jnp.bfloat16)
            sums = jnp.dot(
                jnp.concatenate([upper, lower], axis=1), prefix_ref[...], preferred_element_type=jnp.float32
            )
            taken = jnp.where(inside, jnp.take_along_axis(sums, index, axis=1), 0.0)
            g1 = lax.rem(z + zbins - d1, zbins) * bins + b1
            g2 = lax.rem(z + zbins - d2, zbins) * bins + b2
            first, second = jnp.minimum(g1, g2), jnp.maximum(g1, g2)
            number = first * bins_total - first * (first - 1) // 2 + second - first
            spot = number // pair_share
            line = pl.ds(number - spot * pair_share, 1)
            discs[spot, line, :] += jnp.sum(taken, axis=0, keepdims=True)

    done = [(0, b) for b in range(bins)]
    for at in range(blocks):
        band_sums(at, [(done[i], done[j]) for i in range(bins) for j in range(i, bins)])

    counts = jnp.zeros((1, LANES), jnp.int32)
    for start in range(0, half, LANES):
        every = start + lax.broadcasted_iota(jnp.int32, (LANES, LANES), 0)
        inner = jnp.maximum(2 * edge_reach(lower_edges, every) - 1, 0)
        outer = jnp.maximum(2 * edge_reach(upper_edges, every) - 1, 0)
        counts = counts + jnp.sum(outer - inner, axis=0, keepdims=True)

    for d in range(1, zbins):
        for b in range(bins):
            done.append((d, b))
            for at in range(blocks):
                modes_copies[d, b, at].wait_recv()
                band_sums(at, [(old, (d, b)) for old in done])
    loads[2].wait()

    copies = []
    for n, (dz, df) in enumerate(group):
        target = lax.rem(z + dz, zbins)
        copy = pltpu.make_async_remote_copy(
            src_ref=discs.at[target],
            dst_ref=shares.at[n],
            send_sem=share_ssem.at[n],
            recv_sem=share_rsem.at[n],
            device_id={"zbin": target, "freq": lax.rem(f + df, freqs)},
            device_id_type=MESH,
        )
        copy.start()
        copies.append(copy)
    total = discs[z]
    for n, copy in enumerate(copies):
        copy.wait_recv()
        total = total + shares[n]
    for copy in bank_copies:
        copy.wait_recv()

    shifted = pltpu.roll(total, 1, 1)
    shifted = jnp.where(lax.broadcasted_iota(jnp.int32, total.shape, 1) == 0, 0.0, shifted)
    pseudo = (total - shifted) / (counts.astype(jnp.float32) * float(length * length))
    kind = class_ref[me]
    holder = kind // bank.shape[1]
    matrix = bank[lax.rem(me - holder + patches, patches), kind - holder * bank.shape[1]]
    result = lax.dot_general(
        pseudo,
        matrix,
        (((1,), (1,)), ((), ())),
        precision=lax.Precision.HIGHEST,
        preferred_element_type=jnp.float32,
    )
    for q in range(pair_share):
        out_ref[q] = result[q : q + 1]

    for copy in sum(strip_copies.values(), []) + bank_copies + list(cols_copies.values()) + list(modes_copies.values()) + copies:
        copy.wait_send()


def per_device(density_maps, margin_src, margin_row, margin_count, class_id, coupling_bank, band_edges):
    _, bins, length, columns = density_maps.shape
    half = length // 2
    freqs = lax.axis_size("freq")
    zbins = lax.axis_size("zbin")
    patches = lax.axis_size("patch")
    rows = half // freqs // zbins
    bins_total = bins * zbins
    pair_share = bins_total * (bins_total + 1) // 2 // zbins
    padded = -(-pair_share // 8) * 8
    group = zbins * freqs - 1
    slots = margin_src.shape[1] * W
    blocks = half // LANES

    profile = taper_profile(length, APOD)
    ramp = np.concatenate([profile[:APOD], profile[length - APOD :]])[:, None]
    cos_np, sin_np = fourier_tables(length)
    minus_sin = (-sin_np.astype(np.float32)).astype(ml_dtypes.bfloat16)
    spot = np.arange(half)
    dealt = (spot % rows // BLOCK * (freqs * zbins) + spot // rows) * BLOCK + spot % BLOCK
    table = np.concatenate([cos_np[dealt], minus_sin[dealt]], axis=0)
    turn = np.stack(
        [
            np.concatenate([cos_np.T[:, at : at + LANES], sin_np.T[:, at : at + LANES]], axis=1)
            for at in range(0, half, LANES)
        ]
    )
    ones = np.triu(np.ones((LANES, LANES)))
    prefix = np.concatenate([ones, ones], axis=0).astype(ml_dtypes.bfloat16)

    smem = pl.BlockSpec(memory_space=pltpu.SMEM)
    vmem = pl.BlockSpec(memory_space=pltpu.VMEM)
    anywhere = pl.BlockSpec(memory_space=pl.ANY)
    dma = pltpu.SemaphoreType.DMA
    bf16, f32 = jnp.bfloat16, jnp.float32
    sizes = (patches, zbins, freqs)
    spectra = pl.pallas_call(
        lambda *refs: kernel(sizes, *refs),
        out_shape=jax.ShapeDtypeStruct((pair_share, 1, LANES), f32),
        in_specs=[smem] * 4 + [vmem] * 4 + [anywhere] * 4,
        out_specs=vmem,
        scratch_shapes=[
            pltpu.VMEM((bins, length, columns), bf16),
            pltpu.VMEM((length, length), bf16),
            pltpu.VMEM((blocks, length, 2 * LANES), bf16),
            [pltpu.VMEM((4, W, columns), bf16)] * bins,
            pltpu.VMEM((patches,) + coupling_bank.shape, f32),
            pltpu.VMEM((bins, length, columns), bf16),
            pltpu.VMEM((2, bins, 2 * rows, columns), f32),
            pltpu.VMEM((length, slots), bf16),
            pltpu.VMEM((bins, slots, columns), bf16),
            pltpu.VMEM((zbins, bins, 2 * rows, columns), bf16),
            pltpu.VMEM((zbins, bins, 2 * rows, columns), bf16),
            pltpu.VMEM((zbins, bins, 2 * rows, columns), bf16),
            pltpu.VMEM((zbins, blocks, bins, 4, rows, LANES), bf16),
            pltpu.VMEM((zbins, blocks, bins, 4, rows, LANES), bf16),
            pltpu.VMEM((zbins, padded, LANES), f32),
            pltpu.VMEM((group, padded, LANES), f32),
            dma((3 + bins,)), dma((bins, 4)), dma((bins, 4)), dma((patches,)), dma((patches,)), dma((zbins, bins)), dma((zbins, bins)),
            dma((zbins, bins * blocks)), dma((zbins, bins * blocks)), dma((group,)), dma((group,)),
        ],
        compiler_params=pltpu.CompilerParams(
            collective_id=0, has_side_effects=True, vmem_limit_bytes=56 * 1024 * 1024
        ),
        name="spectra",
    )(
        margin_src, margin_row, margin_count, class_id, band_edges, jnp.asarray(ramp),
        jnp.asarray(profile)[None, :], jnp.asarray(prefix),
        density_maps, coupling_bank, jnp.asarray(table), jnp.asarray(turn),
    )
    return jnp.transpose(spectra, (1, 0, 2))


def solution(mesh):
    in_specs = (
        P(("groups", "patch"), "zbin", None, "freq"),
        P("groups", None),
        P("groups", None),
        P("groups"),
        P("groups"),
        P("patch", None, None),
        P(),
    )
    out_specs = P(("groups", "patch"), "zbin", None)
    return jax.shard_map(
        per_device, mesh=mesh, in_specs=in_specs, out_specs=out_specs, check_vma=False
    )
```

```python
import math

import jax
import jax.numpy as jnp
import ml_dtypes
import numpy as np
from jax import lax
from jax.experimental import pallas as pl
from jax.experimental.pallas import tpu as pltpu
from jax.sharding import PartitionSpec as P

W = 32
BLOCK = 16
APOD = 64
LANES = 128
MESH = pl.DeviceIdType.MESH


def taper_profile(length, ramp_width):
    position = np.arange(length)
    distance = np.minimum(position, length - 1 - position)
    ramped = 0.5 - 0.5 * np.cos(math.pi * (distance + 0.5) / ramp_width)
    return np.where(distance < ramp_width, ramped, 1.0).astype(np.float32)


def fourier_tables(length):
    half = length // 2
    phases = np.arange(half)[:, None] * np.arange(length)[None, :] % length
    angles = phases * (2.0 * math.pi / length)
    return (
        np.cos(angles).astype(np.float32).astype(ml_dtypes.bfloat16),
        np.sin(angles).astype(np.float32).astype(ml_dtypes.bfloat16),
    )


def edge_reach(edges, wave_rows):
    room = edges * edges - wave_rows * wave_rows
    reach = jnp.sqrt(jnp.maximum(room, 0).astype(jnp.float32)).astype(jnp.int32) - 1
    for _ in range(3):
        reach = reach + (reach * reach < room).astype(jnp.int32)
    return jnp.where(room > 0, reach, 0)


def kernel(
    sizes,
    src_ref, row_ref, count_ref, class_ref, edges_ref, ramp_ref, col_taper_ref, prefix_ref,
    maps_hbm, bank_hbm, table_hbm, turn_hbm,
    out_ref,
    maps, table, turn, strips, bank, tapered,
    waiting, strip_table, strip_rows, cols_send, cols_own, cols_recv, modes_send, modes, discs, shares,
    load_sem, strip_send, strip_recv, bank_send, bank_recv, cols_ssem, cols_rsem,
    modes_ssem, modes_rsem, share_ssem, share_rsem,
):
    patches, zbins, freqs = sizes
    bins, length, columns = maps.shape
    half = length // 2
    rows_freq = half // freqs
    rows = rows_freq // zbins
    bins_total = bins * zbins
    pair_total = bins_total * (bins_total + 1) // 2
    pair_share = pair_total // zbins
    me = lax.axis_index("patch")
    z = lax.axis_index("zbin")
    f = lax.axis_index("freq")
    other = 1 - f
    right, left = lax.rem(me + 1, patches), lax.rem(me + patches - 1, patches)

    loads = [
        pltpu.make_async_copy(table_hbm, table, load_sem.at[0]),
        pltpu.make_async_copy(turn_hbm, turn, load_sem.at[1]),
        pltpu.make_async_copy(bank_hbm, bank.at[0], load_sem.at[2]),
    ]
    map_loads = [pltpu.make_async_copy(maps_hbm.at[0, b], maps.at[b], load_sem.at[3 + b]) for b in range(bins)]
    for load in map_loads[:1] + loads[:1] + map_loads[1:] + loads[1:]:
        load.start()

    group = [(dz, df) for dz in range(zbins) for df in range(freqs) if (dz, df) != (0, 0)]
    barrier = pltpu.get_barrier_semaphore()
    for k in range(1, patches):
        pl.semaphore_signal(barrier, inc=1, device_id={"patch": lax.rem(me + k, patches)}, device_id_type=MESH)
    for dz, df in group:
        pl.semaphore_signal(
            barrier,
            inc=1,
            device_id={"zbin": lax.rem(z + dz, zbins), "freq": lax.rem(f + df, freqs)},
            device_id_type=MESH,
        )
    pl.semaphore_wait(barrier, patches - 1 + len(group))

    strip_copies = {b: [] for b in range(bins)}
    for b in range(bins):
        for side, target in ((0, right), (1, left)):
            for half_side, at in ((0, 0), (1, length - W)):
                slot = side * 2 + half_side
                copy = pltpu.make_async_remote_copy(
                    src_ref=maps_hbm.at[0, b, pl.ds(at, W), :],
                    dst_ref=strips[b].at[slot],
                    send_sem=strip_send.at[b, slot],
                    recv_sem=strip_recv.at[b, slot],
                    device_id={"patch": target},
                    device_id_type=MESH,
                )
                copy.start()
                strip_copies[b].append(copy)

    discs[...] = jnp.zeros_like(discs)
    entries = []
    for k in range(src_ref.shape[1]):
        source = src_ref[me, k]
        side = jnp.where(lax.shift_right_logical(source, 1) == left, 0, 1)
        entries.append((side * 2 + (source & 1), k < count_ref[me], row_ref[me, k]))
    def entry_rows(shape, axis):
        place = lax.broadcasted_iota(jnp.int32, shape, axis)
        rows_at = jnp.full(shape, -1, jnp.int32)
        for k, (_, live, row) in enumerate(entries):
            rows_at = jnp.where((place // W == k) & live, row + place % W, rows_at)
        return rows_at

    slots = len(entries) * W
    col_taper = col_taper_ref[:, pl.ds(pl.multiple_of(f * columns, columns), columns)]
    bounds = [0, APOD] + list(range(4 * APOD, length - APOD, 4 * APOD)) + [length - APOD, length]

    def taper(b):
        map_loads[b].wait()
        for start, stop in zip(bounds[:-1], bounds[1:]):
            image = maps[b, pl.ds(start, stop - start), :].astype(jnp.float32)
            if start == 0:
                image = image * ramp_ref[pl.ds(0, APOD), :]
            if stop == length:
                image = image * ramp_ref[pl.ds(APOD, APOD), :]
            tapered[b, pl.ds(start, stop - start), :] = (image * col_taper).astype(jnp.bfloat16)

    order = list(range(1, zbins)) + [0]
    blocks = half // LANES
    spread = freqs * zbins * BLOCK
    heights = [
        BLOCK * sum((at * LANES) ** 2 + (t * spread) ** 2 < (half - 1) ** 2 for t in range(rows // BLOCK))
        for at in range(blocks)
    ]
    def rows_of(ref, half_index, d):
        base = half_index * rows_freq + lax.rem(z + d, zbins) * rows
        return jnp.concatenate(
            [
                ref[pl.ds(pl.multiple_of(base, rows), rows), :],
                ref[pl.ds(pl.multiple_of(half + base, rows), rows), :],
            ],
            axis=0,
        )

    def base_product(half_index, d, b):
        return jnp.dot(rows_of(table, half_index, d), tapered[b], preferred_element_type=jnp.float32)

    def strip_product(half_index, d, b):
        return jnp.dot(rows_of(strip_table, half_index, d), strip_rows[b], preferred_element_type=jnp.float32)

    def prepare(b):
        taper(b)
        if b == 0:
            loads[0].wait()
        for part, half_index in enumerate((other, f)):
            waiting[part, b] = base_product(half_index, early, b)

    def take_strips(b):
        for copy in strip_copies[b]:
            copy.wait_recv()
        for k, (slot, _, _) in enumerate(entries):
            strip = strips[b][slot].astype(jnp.float32) * strip_taper[k * W : (k + 1) * W]
            strip_rows[b, pl.ds(k * W, W), :] = (strip * col_taper).astype(jnp.bfloat16)

    early = order[0]
    across = lax.broadcasted_iota(jnp.int32, (slots, length), 1)
    found = across == entry_rows((slots, 1), 0)
    strip_taper = jnp.sum(jnp.where(found, col_taper_ref[...], 0.0), axis=1, keepdims=True)
    prepare(0)
    pixel = lax.broadcasted_iota(jnp.int32, (length, slots), 0)
    pick = (pixel == entry_rows((1, slots), 1)).astype(jnp.float32).astype(jnp.bfloat16)
    strip_table[...] = jnp.dot(table[...], pick, preferred_element_type=jnp.float32).astype(jnp.bfloat16)

    def near_product(d, b, at):
        own = pl.ds(pl.multiple_of(f * columns, columns), columns)
        return jnp.dot(cols_own[d, b], turn[at, own, :], preferred_element_type=jnp.float32)

    def second_transform(d, b, at, target, near):
        far = pl.ds(pl.multiple_of(other * columns, columns), columns)
        both = near + jnp.dot(
            cols_recv[d, b], turn[at, far, :], preferred_element_type=jnp.float32
        )
        real_cos, real_sin = both[:rows, :LANES], both[:rows, LANES:]
        imag_cos, imag_sin = both[rows:, :LANES], both[rows:, LANES:]
        target[d, at, b, 0] = (real_cos + imag_sin).astype(jnp.bfloat16)
        target[d, at, b, 1] = (real_cos - imag_sin).astype(jnp.bfloat16)
        target[d, at, b, 2] = (imag_cos - real_sin).astype(jnp.bfloat16)
        target[d, at, b, 3] = (imag_cos + real_sin).astype(jnp.bfloat16)

    cols_copies, modes_copies = {}, {}

    def send_cols(d, b):
        copy = pltpu.make_async_remote_copy(
            src_ref=cols_send.at[d, b],
            dst_ref=cols_recv.at[d, b],
            send_sem=cols_ssem.at[d, b],
            recv_sem=cols_rsem.at[d, b],
            device_id={"freq": other},
            device_id_type=MESH,
        )
        copy.start()
        cols_copies[d, b] = copy

    def exchange_cols(d, b):
        base = waiting[0, b] if d == early else base_product(other, d, b)
        cols_send[d, b] = (base + strip_product(other, d, b)).astype(jnp.bfloat16)
        send_cols(d, b)
        base = waiting[1, b] if d == early else base_product(f, d, b)
        cols_own[d, b] = (base + strip_product(f, d, b)).astype(jnp.bfloat16)

    def make_modes(d, b):
        near = near_product(d, b, 0)
        cols_copies[d, b].wait_recv()
        for at in range(blocks):
            if at:
                near = near_product(d, b, at)
            second_transform(d, b, at, modes_send if d else modes, near)
            if d:
                part = pl.ds(0, heights[at])
                copy = pltpu.make_async_remote_copy(
                    src_ref=modes_send.at[d, at, b, :, part, :],
                    dst_ref=modes.at[d, at, b, :, part, :],
                    send_sem=modes_ssem.at[d, b * blocks + at],
                    recv_sem=modes_rsem.at[d, b * blocks + at],
                    device_id={"zbin": lax.rem(z + d, zbins)},
                    device_id_type=MESH,
                )
                copy.start()
                modes_copies[d, b, at] = copy

    for d in order:
        for b in range(bins):
            if d == early:
                take_strips(b)
            exchange_cols(d, b)
            if d == early and b == 0:
                loads[1].wait()
            make_modes(d, b)
            if d == early and b + 1 < bins:
                prepare(b + 1)

    bank_copies = []
    for k in range(1, patches):
        copy = pltpu.make_async_remote_copy(
            src_ref=bank_hbm,
            dst_ref=bank.at[k],
            send_sem=bank_send.at[k],
            recv_sem=bank_recv.at[k],
            device_id={"patch": lax.rem(me + k, patches)},
            device_id_type=MESH,
        )
        copy.start()
        bank_copies.append(copy)

    local_row = lax.broadcasted_iota(jnp.int32, (rows, LANES), 0)
    wave_rows = (local_row // BLOCK * (freqs * zbins) + f * zbins + z) * BLOCK + local_row % BLOCK
    lane = lax.broadcasted_iota(jnp.int32, (rows, LANES), 1)
    lower_edges = edges_ref[pl.ds(0, LANES)].reshape(1, LANES)
    upper_edges = edges_ref[pl.ds(1, LANES)].reshape(1, LANES)
    low = lower_edges[:, :1]
    reach = edge_reach(upper_edges, wave_rows)

    def band_sums(at, pairs):
        height = heights[at]
        index = (jnp.clip(reach - at * LANES, 1, LANES) - 1)[:height]
        inside = (reach > at * LANES)[:height]
        wave_cols = lane + at * LANES
        scale = (wave_rows * wave_rows + wave_cols * wave_cols >= low * low).astype(jnp.float32)
        if at == 0:
            scale = scale * jnp.where(lane == 0, 0.5, 1.0)
        scale = scale[:height]
        part = pl.ds(0, height)
        for (d1, b1), (d2, b2) in pairs:
            cross = None
            for c in range(4):
                term = modes[d1, at, b1, c, part, :].astype(jnp.float32) * modes[d2, at, b2, c, part, :].astype(
                    jnp.float32
                )
                cross = term if cross is None else cross + term
            cross = cross * scale
            upper = cross.astype(jnp.bfloat16)
            lower = (cross - upper.astype(jnp.float32)).astype(jnp.bfloat16)
            sums = jnp.dot(
                jnp.concatenate([upper, lower], axis=1), prefix_ref[...], preferred_element_type=jnp.float32
            )
            taken = jnp.where(inside, jnp.take_along_axis(sums, index, axis=1), 0.0)
            g1 = lax.rem(z + zbins - d1, zbins) * bins + b1
            g2 = lax.rem(z + zbins - d2, zbins) * bins + b2
            first, second = jnp.minimum(g1, g2), jnp.maximum(g1, g2)
            number = first * bins_total - first * (first - 1) // 2 + second - first
            spot = number // pair_share
            line = pl.ds(number - spot * pair_share, 1)
            discs[spot, line, :] += jnp.sum(taken, axis=0, keepdims=True)

    done = [(0, b) for b in range(bins)]
    for at in range(blocks):
        band_sums(at, [(done[i], done[j]) for i in range(bins) for j in range(i, bins)])

    counts = jnp.zeros((1, LANES), jnp.int32)
    for start in range(0, half, LANES):
        every = start + lax.broadcasted_iota(jnp.int32, (LANES, LANES), 0)
        inner = jnp.maximum(2 * edge_reach(lower_edges, every) - 1, 0)
        outer = jnp.maximum(2 * edge_reach(upper_edges, every) - 1, 0)
        counts = counts + jnp.sum(outer - inner, axis=0, keepdims=True)

    for d in range(1, zbins):
        for b in range(bins):
            done.append((d, b))
            for at in range(blocks):
                modes_copies[d, b, at].wait_recv()
                band_sums(at, [(old, (d, b)) for old in done])
    loads[2].wait()

    copies = []
    for n, (dz, df) in enumerate(group):
        target = lax.rem(z + dz, zbins)
        copy = pltpu.make_async_remote_copy(
            src_ref=discs.at[target],
            dst_ref=shares.at[n],
            send_sem=share_ssem.at[n],
            recv_sem=share_rsem.at[n],
            device_id={"zbin": target, "freq": lax.rem(f + df, freqs)},
            device_id_type=MESH,
        )
        copy.start()
        copies.append(copy)
    total = discs[z]
    for n, copy in enumerate(copies):
        copy.wait_recv()
        total = total + shares[n]
    for copy in bank_copies:
        copy.wait_recv()

    shifted = pltpu.roll(total, 1, 1)
    shifted = jnp.where(lax.broadcasted_iota(jnp.int32, total.shape, 1) == 0, 0.0, shifted)
    pseudo = (total - shifted) / (counts.astype(jnp.float32) * float(length * length))
    kind = class_ref[me]
    holder = kind // bank.shape[1]
    matrix = bank[lax.rem(me - holder + patches, patches), kind - holder * bank.shape[1]]
    result = lax.dot_general(
        pseudo,
        matrix,
        (((1,), (1,)), ((), ())),
        precision=lax.Precision.HIGHEST,
        preferred_element_type=jnp.float32,
    )
    for q in range(pair_share):
        out_ref[q] = result[q : q + 1]

    for copy in sum(strip_copies.values(), []) + bank_copies + list(cols_copies.values()) + list(modes_copies.values()) + copies:
        copy.wait_send()


def per_device(density_maps, margin_src, margin_row, margin_count, class_id, coupling_bank, band_edges):
    _, bins, length, columns = density_maps.shape
    half = length // 2
    freqs = lax.axis_size("freq")
    zbins = lax.axis_size("zbin")
    patches = lax.axis_size("patch")
    rows = half // freqs // zbins
    bins_total = bins * zbins
    pair_share = bins_total * (bins_total + 1) // 2 // zbins
    padded = -(-pair_share // 8) * 8
    group = zbins * freqs - 1
    slots = margin_src.shape[1] * W
    blocks = half // LANES

    profile = taper_profile(length, APOD)
    ramp = np.concatenate([profile[:APOD], profile[length - APOD :]])[:, None]
    cos_np, sin_np = fourier_tables(length)
    minus_sin = (-sin_np.astype(np.float32)).astype(ml_dtypes.bfloat16)
    spot = np.arange(half)
    dealt = (spot % rows // BLOCK * (freqs * zbins) + spot // rows) * BLOCK + spot % BLOCK
    table = np.concatenate([cos_np[dealt], minus_sin[dealt]], axis=0)
    turn = np.stack(
        [
            np.concatenate([cos_np.T[:, at : at + LANES], sin_np.T[:, at : at + LANES]], axis=1)
            for at in range(0, half, LANES)
        ]
    )
    ones = np.triu(np.ones((LANES, LANES)))
    prefix = np.concatenate([ones, ones], axis=0).astype(ml_dtypes.bfloat16)

    smem = pl.BlockSpec(memory_space=pltpu.SMEM)
    vmem = pl.BlockSpec(memory_space=pltpu.VMEM)
    anywhere = pl.BlockSpec(memory_space=pl.ANY)
    dma = pltpu.SemaphoreType.DMA
    bf16, f32 = jnp.bfloat16, jnp.float32
    sizes = (patches, zbins, freqs)
    spectra = pl.pallas_call(
        lambda *refs: kernel(sizes, *refs),
        out_shape=jax.ShapeDtypeStruct((pair_share, 1, LANES), f32),
        in_specs=[smem] * 4 + [vmem] * 4 + [anywhere] * 4,
        out_specs=vmem,
        scratch_shapes=[
            pltpu.VMEM((bins, length, columns), bf16),
            pltpu.VMEM((length, length), bf16),
            pltpu.VMEM((blocks, length, 2 * LANES), bf16),
            [pltpu.VMEM((4, W, columns), bf16)] * bins,
            pltpu.VMEM((patches,) + coupling_bank.shape, f32),
            pltpu.VMEM((bins, length, columns), bf16),
            pltpu.VMEM((2, bins, 2 * rows, columns), f32),
            pltpu.VMEM((length, slots), bf16),
            pltpu.VMEM((bins, slots, columns), bf16),
            pltpu.VMEM((zbins, bins, 2 * rows, columns), bf16),
            pltpu.VMEM((zbins, bins, 2 * rows, columns), bf16),
            pltpu.VMEM((zbins, bins, 2 * rows, columns), bf16),
            pltpu.VMEM((zbins, blocks, bins, 4, rows, LANES), bf16),
            pltpu.VMEM((zbins, blocks, bins, 4, rows, LANES), bf16),
            pltpu.VMEM((zbins, padded, LANES), f32),
            pltpu.VMEM((group, padded, LANES), f32),
            dma((3 + bins,)), dma((bins, 4)), dma((bins, 4)), dma((patches,)), dma((patches,)), dma((zbins, bins)), dma((zbins, bins)),
            dma((zbins, bins * blocks)), dma((zbins, bins * blocks)), dma((group,)), dma((group,)),
        ],
        compiler_params=pltpu.CompilerParams(
            collective_id=0, has_side_effects=True, vmem_limit_bytes=56 * 1024 * 1024
        ),
        name="spectra",
    )(
        margin_src, margin_row, margin_count, class_id, band_edges, jnp.asarray(ramp),
        jnp.asarray(profile)[None, :], jnp.asarray(prefix),
        density_maps, coupling_bank, jnp.asarray(table), jnp.asarray(turn),
    )
    return jnp.transpose(spectra, (1, 0, 2))


def solution(mesh):
    in_specs = (
        P(("groups", "patch"), "zbin", None, "freq"),
        P("groups", None),
        P("groups", None),
        P("groups"),
        P("groups"),
        P("patch", None, None),
        P(),
    )
    out_specs = P(("groups", "patch"), "zbin", None)
    return jax.shard_map(
        per_device, mesh=mesh, in_specs=in_specs, out_specs=out_specs, check_vma=False
    )
```
